128 devices in a mesh: row: 8 (over x, z_hi), col: 16 (over z_lo, y, core).
Axes of the slice: x: 4, y: 4, z: 4 (z_hi: 2, z_lo: 2; z = z_hi * 2 + z_lo), core: 2. Of those that a mesh axis runs over, the one named last changes fastest.
Arguments:
- tokens: bfloat16 [1024, 6144], P('row', 'col'), may hold values from -6 to 6
- w_in: bfloat16 [6144, 24576], P('col', 'row'), may hold values from -0.078125 to 0.078125
- w_out: bfloat16 [24576, 6144], P('row', 'col'), may hold values from -0.0390625 to 0.0390625
- out_grad: bfloat16 [1024, 6144], P('row', 'col'), may hold values from -6 to 6
Outputs:
- mlp_out: bfloat16 [1024, 6144], P('row', 'col')
- in_grad: bfloat16 [1024, 6144], P('row', 'col')
- w_in_grad: float32 [6144, 24576], P('col', 'row')
- w_out_grad: float32 [24576, 6144], P('row', 'col')
The draws below stay inside these ranges and needn't reach their ends.
All inputs are finite; a program needn't handle non-finite values.
Results may differ from the reference program's by a relative error of at most 0.005.
Values may be sent and summed in bfloat16 or wider, within the bound.
A program may use at most 128 MiB of HBM per device.

```python
import jax
import jax.numpy as jnp
from jax import lax

D = 6144
FF = 24576
TOKENS = 1024


def block_scale(own_key, shape, shards, smallest, high):
    gain, own = 1.0, jax.random.fold_in(own_key, 6)
    for axis_at, parts in shards:
        steps = jnp.exp(jax.random.uniform(jax.random.fold_in(own, axis_at), (parts,), jnp.float32, smallest / len(shards), high / len(shards)))
        gain = gain * jnp.repeat(steps, shape[axis_at] // parts).reshape([-1 if axis == axis_at else 1 for axis in range(len(shape))])
    return gain


def normal_values(stream_key, extent, deviation, reach, cuts=(), dtype=jnp.bfloat16):
    values = jax.random.normal(stream_key, extent, jnp.float32) * deviation
    if len(cuts) > 0:
        values = block_scale(stream_key, extent, cuts, -0.22, 0.18) * values
    return jnp.clip(values, min=-reach, max=reach).astype(dtype)


def setup_inputs(seed: int = 0) -> dict:
    arg_keys = jax.random.split(jax.random.key(seed), 5)
    tokens = normal_values(arg_keys[0], (TOKENS, D), 1.0, 6.0, ((0, 8), (1, 16)))
    w_in = normal_values(arg_keys[1], (D, FF), D ** -0.5, 0.078125, ((0, 16), (1, 8)))
    w_out = normal_values(arg_keys[2], (FF, D), FF ** -0.5, 0.0390625, ((0, 8), (1, 16)))
    out_grad = normal_values(arg_keys[3], (TOKENS, D), 1.0, 6.0, ((0, 8), (1, 16)))
    return dict(tokens=tokens, w_in=w_in, w_out=w_out, out_grad=out_grad)


sqrt_half = 0.7071067811865476
inv_root = 0.3989422804014327

def gelu_value(value):
    return 0.5 * value * (1.0 + jax.scipy.special.erf(value * sqrt_half))

def gelu_slope(value):
    return 0.5 * (1.0 + jax.scipy.special.erf(value * sqrt_half)) + value * jnp.exp(-0.5 * value * value) * inv_root

def product(left, right):
    return jnp.dot(left, right, precision=lax.Precision.HIGHEST, preferred_element_type=jnp.float32)

def reference(tokens, w_in, w_out, out_grad):
    x_float = tokens.astype(jnp.float32)
    w_in_float = w_in.astype(jnp.float32)
    w_out_float = w_out.astype(jnp.float32)
    grad_float = out_grad.astype(jnp.float32)
    preact = product(x_float, w_in_float)
    hidden = gelu_value(preact).astype(jnp.bfloat16)
    hidden_float = hidden.astype(jnp.float32)
    mlp_out = product(hidden_float, w_out_float).astype(jnp.bfloat16)
    w_out_grad = product(hidden_float.T, grad_float)
    hidden_grad = product(grad_float, w_out_float.T)
    preact_grad = (hidden_grad * gelu_slope(preact)).astype(jnp.bfloat16)
    preact_float = preact_grad.astype(jnp.float32)
    in_grad = product(preact_float, w_in_float.T).astype(jnp.bfloat16)
    w_in_grad = product(x_float.T, preact_float)
    return (mlp_out, in_grad, w_in_grad, w_out_grad)
```

```python
import jax
import jax.numpy as jnp
from jax import lax
from jax.experimental import pallas as pl
from jax.experimental.pallas import tpu as pltpu
from jax.sharding import PartitionSpec as P

MESH = pl.DeviceIdType.MESH
f32, bf16 = jnp.float32, jnp.bfloat16
sqrt_half = 0.7071067811865476
inv_root = 0.3989422804014327

ROWS = 8
TOK = 128
DL = 384
DC = 768
FL = 3072
FH = 1536
NCH = 8
B = TOK // NCH
C = B * ROWS
WA, WB = 1024, 512
HA, HB = WA // 2, WB // 2
STAGES = 13

(AGZ, AGX, AGC, A_REL, A_DIR, A_SUM, A_Z, B_Z, B_REL, B_DIR, B_SUM, GA_Z, GA_1, GA_2, GB_1, GB_2, GB_Z, GC, RX, RZ) = range(20)
KINDS = 20


def kernel(
    tok, dy, w_in, w_out,
    mlp, ing, wig, wog,
    xall, wih, woh, winv, woutv, part,
    a_rel, a_dir, a_sum, a_out, a_z, b_z, b_rel, b_dir, b_sum,
    hid, oc, xr, xs, zr, g_in, g_out,
    ssem, rsem, wsem, lsem,
):
    row, col = lax.axis_index("row"), lax.axis_index("col")
    x, zh = row // 2, row % 2
    zl, y, core = col // 8, (col // 2) % 4, col % 2
    other = 1 - core

    def dev(dx=0, dzh=0, dzl=0, dyy=0, dc=0):
        return (
            ((x + dx) % 4) * 2 + (zh + dzh) % 2,
            (((zl + dzl) % 2) * 4 + (y + dyy) % 4) * 2 + (core + dc) % 2,
        )

    XP, XM, XO = dev(dx=1), dev(dx=3), dev(dx=2)
    ZH, ZL = dev(dzh=1), dev(dzl=1)
    YP, YM = dev(dyy=1), dev(dyy=3)
    CO = dev(dc=1)
    yr, yl, yo = (y + 1) % 4, (y + 3) % 4, (y + 2) % 4

    def send(src, dst, c, kind, to):
        pltpu.make_async_remote_copy(
            src_ref=src, dst_ref=dst, send_sem=ssem.at[c, kind], recv_sem=rsem.at[c, kind],
            device_id=to, device_id_type=MESH,
        ).start()

    def got(view, c, kind):
        pltpu.make_async_copy(view, view, rsem.at[c, kind]).wait()

    def sent(view, c, kind):
        pltpu.make_async_copy(view, view, ssem.at[c, kind]).wait()

    def ds(i, size):
        return pl.ds(pl.multiple_of(i * size, size), size)

    barrier = pltpu.get_barrier_semaphore()
    for d in (XP, XM, XO, ZH, ZL, YP, YM, CO):
        pl.semaphore_signal(barrier, 1, device_id=d, device_id_type=MESH)
    pl.semaphore_wait(barrier, 8)

    swaps = [
        pltpu.make_async_remote_copy(
            src_ref=w_in.at[:, ds(other, FH)], dst_ref=wih.at[pl.ds(DL, DL), :],
            send_sem=wsem.at[0], recv_sem=wsem.at[1], device_id=CO, device_id_type=MESH,
        ),
        pltpu.make_async_remote_copy(
            src_ref=w_out.at[ds(other, FH), :], dst_ref=woh.at[:, pl.ds(DL, DL)],
            send_sem=wsem.at[2], recv_sem=wsem.at[3], device_id=CO, device_id_type=MESH,
        ),
    ]
    locals_ = [
        pltpu.make_async_copy(w_in.at[:, ds(core, FH)], wih.at[pl.ds(0, DL), :], lsem.at[0]),
        pltpu.make_async_copy(w_out.at[ds(core, FH), :], woh.at[:, pl.ds(0, DL)], lsem.at[1]),
        pltpu.make_async_copy(w_in, winv, lsem.at[2]),
        pltpu.make_async_copy(w_out, woutv, lsem.at[3]),
    ]
    results = [
        pltpu.make_async_copy(g_out, wog, lsem.at[4]),
        pltpu.make_async_copy(g_in, wig, lsem.at[5]),
    ]

    def s0(c):
        mine = ds(row, B)
        xall[c, 0, mine, 0:DL] = tok[ds(c, B), :]
        xall[c, 1, mine, 0:DL] = dy[ds(c, B), :]
        view = xall.at[c, :, mine, 0:DL]
        send(view, view, c, AGZ, ZH)
        for to in (XP, XM, XO):
            send(view, view, c, AGX, to)

    def s1(c):
        view = xall.at[c, :, ds(x * 2 + 1 - zh, B), 0:DL]
        got(view, c, AGZ)
        for to in (XP, XM, XO):
            send(view, view, c, AGX, to)

    def s2(c):
        got(xall.at[c, :, 0 : 6 * B, 0:DL], c, AGX)
        send(xall.at[c, :, :, 0:DL], xall.at[c, :, :, DL:DC], c, AGC, CO)

    def y_rows(d, rows, off):
        return pl.ds(pl.multiple_of(d * rows + off, B), rows)

    def y_send(c, rows, off, c0, h, rel, direct, krel, kdir):
        first, second = pl.ds(c0, h), pl.ds(c0 + h, h)
        send(part.at[c, :, y_rows(yo, rows, off), first], rel.at[c, 0], c, krel, YP)
        send(part.at[c, :, y_rows(yo, rows, off), second], rel.at[c, 1], c, krel, YM)
        send(part.at[c, :, y_rows(yr, rows, off), second], direct.at[c, 0], c, kdir, YP)
        send(part.at[c, :, y_rows(yl, rows, off), first], direct.at[c, 1], c, kdir, YM)

    def y_relay(c, rows, off, c0, h, rel, total, krel, ksum):
        got(rel.at[c], c, krel)
        for i, (d, to) in enumerate(((yr, YP), (yl, YM))):
            place = (c, slice(None), y_rows(d, rows, off), pl.ds(c0 + i * h, h))
            part[place] = (part[place].astype(f32) + rel[c, i].astype(f32)).astype(bf16)
            send(part.at[place], total.at[c, i], c, ksum, to)

    def y_total(c, rows, off, sub, c0, h, direct, total, i):
        own = part[c, :, pl.ds(pl.multiple_of(y * rows + off + sub, B), B), pl.ds(c0 + i * h, h)]
        at = pl.ds(pl.multiple_of(sub, B), B)
        return own.astype(f32) + direct[c, 1 - i, :, at, :].astype(f32) + total[c, i, :, at, :].astype(f32)

    off_b = zl * (4 * B)
    a_mine, b_mine = ds(y * 2 + zl, B), ds(zl * 4 + y, B)

    def s3(c):
        @pl.when(c == 0)
        def _():
            for copy in locals_[:2]:
                copy.wait()
            for copy in swaps:
                copy.wait_recv()

        got(xall.at[c, :, :, DL:DC], c, AGC)

        @pl.loop(0, FH // 256)
        def _(j):
            cols = ds(j, 256)
            part[c, 0, :, cols] = jnp.dot(
                xall[c, 0], wih[:, cols], preferred_element_type=f32
            ).astype(bf16)
            part[c, 1, :, cols] = lax.dot_general(
                xall[c, 1], woh[cols, :], (((1,), (1,)), ((), ())), preferred_element_type=f32
            ).astype(bf16)

        y_send(c, 2 * B, 0, 0, HA, a_rel, a_dir, A_REL, A_DIR)
        send(part.at[c, :, ds(1 - zl, 4 * B), WA:FH], b_z.at[c], c, B_Z, ZL)

    def s4(c):
        y_relay(c, 2 * B, 0, 0, HA, a_rel, a_sum, A_REL, A_SUM)
        got(b_z.at[c], c, B_Z)
        place = (c, slice(None), ds(zl, 4 * B), slice(WA, FH))
        part[place] = (part[place].astype(f32) + b_z[c].astype(f32)).astype(bf16)
        y_send(c, B, off_b, WA, HB, b_rel, b_dir, B_REL, B_DIR)

    def s5(c):
        got(a_dir.at[c], c, A_DIR)
        got(a_sum.at[c], c, A_SUM)
        for i in range(2):
            a_out[c, :, :, i * HA : (i + 1) * HA] = y_total(
                c, 2 * B, 0, (1 - zl) * B, 0, HA, a_dir, a_sum, i
            ).astype(bf16)
        send(a_out.at[c], a_z.at[c], c, A_Z, ZL)
        y_relay(c, B, off_b, WA, HB, b_rel, b_sum, B_REL, B_SUM)

    def unit(c, rows, c0, h, pre, grad):
        half_erf = 0.5 * (1.0 + lax.erf(pre * sqrt_half))
        hid[core, c, 0, rows, c0 : c0 + h] = (pre * half_erf).astype(bf16)
        slope = half_erf + pre * jnp.exp(-0.5 * pre * pre) * inv_root
        hid[core, c, 1, rows, c0 : c0 + h] = (grad * slope).astype(bf16)

    def s6(c):
        got(a_z.at[c], c, A_Z)
        for i in range(2):
            both = y_total(c, 2 * B, 0, zl * B, 0, HA, a_dir, a_sum, i)
            both = both + a_z[c, :, :, i * HA : (i + 1) * HA].astype(f32)
            unit(c, a_mine, i * HA, HA, both[0], both[1])
        view = hid.at[core, c, :, a_mine, 0:WA]
        send(view, view, c, GA_Z, ZL)
        got(b_dir.at[c], c, B_DIR)
        got(b_sum.at[c], c, B_SUM)
        for i in range(2):
            both = y_total(c, B, off_b, 0, WA, HB, b_dir, b_sum, i)
            unit(c, b_mine, WA + i * HB, HB, both[0], both[1])
        view = hid.at[core, c, :, b_mine, WA:FH]
        send(view, view, c, GB_1, YP)
        send(view, view, c, GB_1, YM)

    def y_forward(c, rows, off, c0, h, kind):
        for i, (d, to) in enumerate(((yl, YP), (yr, YM))):
            view = hid.at[core, c, :, y_rows(d, rows, off), pl.ds(c0 + i * h, h)]
            send(view, view, c, kind, to)

    def s7(c):
        got(hid.at[core, c, :, ds(y * 2 + 1 - zl, B), 0:WA], c, GA_Z)
        view = hid.at[core, c, :, ds(y, 2 * B), 0:WA]
        send(view, view, c, GA_1, YP)
        send(view, view, c, GA_1, YM)
        got(hid.at[core, c, :, 0 : 2 * B, WA:FH], c, GB_1)
        y_forward(c, B, off_b, WA, HB, GB_2)

    def s8(c):
        got(hid.at[core, c, :, 0 : 4 * B, 0:WA], c, GA_1)
        y_forward(c, 2 * B, 0, 0, HA, GA_2)
        got(hid.at[core, c, :, 0:B, WA:FH], c, GB_2)
        view = hid.at[core, c, :, ds(zl, 4 * B), WA:FH]
        send(view, view, c, GB_Z, ZL)

    def s9(c):
        got(hid.at[core, c, :, 0 : 2 * B, 0:WA], c, GA_2)
        got(hid.at[core, c, :, 0 : 4 * B, WA:FH], c, GB_Z)
        send(hid.at[core, c], hid.at[core, c], c, GC, CO)

    def s10(c):
        @pl.when(c == 0)
        def _():
            for copy in locals_[2:]:
                copy.wait()

        got(hid.at[other, c], c, GC)
        for k in range(2):
            units = pl.ds(k * FH, FH)
            out = jnp.dot(hid[k, c, 0], woutv[units, :], preferred_element_type=f32)
            back = lax.dot_general(
                hid[k, c, 1], winv[:, units], (((1,), (1,)), ((), ())), preferred_element_type=f32
            )
            if k == 0:
                oc[c, 0], oc[c, 1] = out, back
            else:
                oc[c, 0] += out
                oc[c, 1] += back
        for i, (d, to) in enumerate((((x + 1) % 4, XP), ((x + 3) % 4, XM), ((x + 2) % 4, XO))):
            send(oc.at[c, :, ds(d, 2 * B), :], xr.at[c, i], c, RX, to)

        @pl.when(c % 2 == 1)
        def _():
            pair = pl.ds(c - 1, 2)
            tn = (((0,), (0,)), ((), ()))
            for k in range(2):

                @pl.loop(0, FH // 256)
                def _(j):
                    units = hid[k, pair, 0, :, ds(j, 256)].reshape(2 * C, 256)
                    down = xall[pair, 1, :, 0:DL].reshape(2 * C, DL)
                    g_out[ds(k * (FH // 256) + j, 256), :] += lax.dot_general(
                        units, down, tn, preferred_element_type=f32
                    )

            @pl.when(c == NCH - 1)
            def _():
                results[0].start()

            for k in range(2):

                @pl.loop(0, FH // 256)
                def _(j):
                    units = hid[k, pair, 1, :, ds(j, 256)].reshape(2 * C, 256)
                    up = xall[pair, 0, :, 0:DL].reshape(2 * C, DL)
                    g_in[:, ds(k * (FH // 256) + j, 256)] += lax.dot_general(
                        up, units, tn, preferred_element_type=f32
                    )

            @pl.when(c == NCH - 1)
            def _():
                results[1].start()

    def x_total(c, z):
        at = ds(z, B)
        total = oc[c, :, pl.ds(pl.multiple_of(x * (2 * B) + z * B, B), B), :]
        for i in range(3):
            total = total + xr[c, i, :, at, :]
        return total

    def s11(c):
        got(xr.at[c], c, RX)
        xs[c] = x_total(c, 1 - zh)
        send(xs.at[c], zr.at[c], c, RZ, ZH)

    def s12(c):
        got(zr.at[c], c, RZ)
        total = x_total(c, zh) + zr[c]
        mlp[ds(c, B), :] = total[0].astype(bf16)
        ing[ds(c, B), :] = total[1].astype(bf16)
        sent(xall.at[c, :, 0:B, 0:DL], c, AGZ)
        sent(xall.at[c, :, 0 : 6 * B, 0:DL], c, AGX)
        sent(xall.at[c, :, :, 0:DL], c, AGC)
        for buf, kind in (
            (a_rel, A_REL), (a_dir, A_DIR), (a_sum, A_SUM), (a_z, A_Z),
            (b_z, B_Z), (b_rel, B_REL), (b_dir, B_DIR), (b_sum, B_SUM), (xr, RX), (zr, RZ),
        ):
            sent(buf.at[c], c, kind)
        for rows, cols, kind in (
            (B, slice(0, WA), GA_Z), (4 * B, slice(0, WA), GA_1), (2 * B, slice(0, WA), GA_2),
            (2 * B, slice(WA, FH), GB_1), (B, slice(WA, FH), GB_2), (4 * B, slice(WA, FH), GB_Z),
        ):
            sent(hid.at[core, c, :, 0:rows, cols], c, kind)
        sent(hid.at[core, c], c, GC)

    for copy in locals_:
        copy.start()
    for copy in swaps:
        copy.start()
    g_in[...] = jnp.zeros_like(g_in)
    g_out[...] = jnp.zeros_like(g_out)

    order = (
        (12, s12), (11, s11), (9, s9), (8, s8), (7, s7), (6, s6), (5, s5), (4, s4),
        (2, s2), (1, s1), (0, s0), (3, s3), (10, s10),
    )

    @pl.loop(0, NCH + STAGES - 1)
    def _(t):
        for stage, work in order:

            @pl.when((t >= stage) & (t < stage + NCH))
            def _(stage=stage, work=work):
                work(t - stage)

    for copy in results:
        copy.wait()
    for copy in swaps:
        copy.wait_send()


def on_device(tokens, w_in, w_out, out_grad):
    vmem, anywhere = pl.BlockSpec(memory_space=pltpu.VMEM), pl.BlockSpec(memory_space=pl.ANY)
    scratch = [
        ((NCH, 2, C, DC), bf16),
        ((DC, FH), bf16),
        ((FH, DC), bf16),
        ((DL, FL), bf16),
        ((FL, DL), bf16),
        ((NCH, 2, C, FH), bf16),
        ((NCH, 2, 2, 2 * B, HA), bf16),
        ((NCH, 2, 2, 2 * B, HA), bf16),
        ((NCH, 2, 2, 2 * B, HA), bf16),
        ((NCH, 2, B, WA), bf16),
        ((NCH, 2, B, WA), bf16),
        ((NCH, 2, 4 * B, WB), bf16),
        ((NCH, 2, 2, B, HB), bf16),
        ((NCH, 2, 2, B, HB), bf16),
        ((NCH, 2, 2, B, HB), bf16),
        ((2, NCH, 2, C, FH), bf16),
        ((NCH, 2, C, DL), f32),
        ((NCH, 3, 2, 2 * B, DL), f32),
        ((NCH, 2, B, DL), f32),
        ((NCH, 2, B, DL), f32),
        ((DL, FL), f32),
        ((FL, DL), f32),
    ]
    return pl.pallas_call(
        kernel,
        out_shape=(
            jax.ShapeDtypeStruct((TOK, DL), bf16),
            jax.ShapeDtypeStruct((TOK, DL), bf16),
            jax.ShapeDtypeStruct((DL, FL), f32),
            jax.ShapeDtypeStruct((FL, DL), f32),
        ),
        in_specs=[vmem, vmem, anywhere, anywhere],
        out_specs=(vmem, vmem, anywhere, anywhere),
        scratch_shapes=[pltpu.VMEM(shape, dtype) for shape, dtype in scratch]
        + [
            pltpu.SemaphoreType.DMA((NCH, KINDS)),
            pltpu.SemaphoreType.DMA((NCH, KINDS)),
            pltpu.SemaphoreType.DMA((4,)),
            pltpu.SemaphoreType.DMA((6,)),
        ],
        compiler_params=pltpu.CompilerParams(
            collective_id=0, has_side_effects=True, vmem_limit_bytes=63 * 2**20
        ),
    )(tokens, out_grad, w_in, w_out)


def solution(mesh):
    in_specs = (P("row", "col"), P("col", "row"), P("row", "col"), P("row", "col"))
    out_specs = (P("row", "col"), P("row", "col"), P("col", "row"), P("row", "col"))
    return jax.shard_map(
        on_device, mesh=mesh, in_specs=in_specs, out_specs=out_specs, check_vma=False
    )
```

```python
import jax
import jax.numpy as jnp
from jax import lax
from jax.experimental import pallas as pl
from jax.experimental.pallas import tpu as pltpu
from jax.sharding import PartitionSpec as P

MESH = pl.DeviceIdType.MESH
f32, bf16 = jnp.float32, jnp.bfloat16
sqrt_half = 0.7071067811865476
inv_root = 0.3989422804014327

ROWS = 8
TOK = 128
DL = 384
DC = 768
FL = 3072
FH = 1536
NCH = 8
B = TOK // NCH
C = B * ROWS
WA, WB = 1024, 512
HA, HB = WA // 2, WB // 2
HT = TOK // 2
NEAR = {0: 0, 3: 0, 5: HT, 6: HT}
FAR = (1, 4)
STAGES = 10

(AGX, AGC, A_REL, A_DIR, A_SUM, A_Z, B_Z, B_REL, B_DIR, B_SUM, GA_Z, GA_1, GA_2, GB_1, GB_2, GB_Z, GC, RX, RZ) = range(19)
KINDS = 19


def kernel(
    tok, dy, w_in, w_out,
    mlp, ing, hid_o, xo,
    xall, wih, woh, winv, woutv, part,
    a_rel, a_dir, a_sum, a_out, a_z, b_z, b_rel, b_dir, b_sum,
    hid, oc, xr, zs, zr,
    ssem, rsem, wsem, lsem, hsem,
):
    row, col = lax.axis_index("row"), lax.axis_index("col")
    x, zh = row // 2, row % 2
    zl, y, core = col // 8, (col // 2) % 4, col % 2
    other = 1 - core

    def dev(dx=0, dzh=0, dzl=0, dyy=0, dc=0):
        return (
            ((x + dx) % 4) * 2 + (zh + dzh) % 2,
            (((zl + dzl) % 2) * 4 + (y + dyy) % 4) * 2 + (core + dc) % 2,
        )

    XP, XM, XO = dev(dx=1), dev(dx=3), dev(dx=2)
    ZH, ZL = dev(dzh=1), dev(dzl=1)
    YP, YM = dev(dyy=1), dev(dyy=3)
    CO = dev(dc=1)
    yr, yl, yo = (y + 1) % 4, (y + 3) % 4, (y + 2) % 4

    def send(src, dst, c, kind, to):
        pltpu.make_async_remote_copy(
            src_ref=src, dst_ref=dst, send_sem=ssem.at[c, kind], recv_sem=rsem.at[c, kind],
            device_id=to, device_id_type=MESH,
        ).start()

    def got(view, c, kind):
        pltpu.make_async_copy(view, view, rsem.at[c, kind]).wait()

    def sent(view, c, kind):
        pltpu.make_async_copy(view, view, ssem.at[c, kind]).wait()

    def ds(i, size):
        return pl.ds(pl.multiple_of(i * size, size), size)

    barrier = pltpu.get_barrier_semaphore()
    for d in (XP, XM, XO, ZH, ZL, YP, YM, CO):
        pl.semaphore_signal(barrier, 1, device_id=d, device_id_type=MESH)
    pl.semaphore_wait(barrier, 8)

    swaps = [
        pltpu.make_async_remote_copy(
            src_ref=w_in.at[:, ds(other, FH)], dst_ref=wih.at[pl.ds(DL, DL), :],
            send_sem=wsem.at[0], recv_sem=wsem.at[1], device_id=CO, device_id_type=MESH,
        ),
        pltpu.make_async_remote_copy(
            src_ref=w_out.at[ds(other, FH), :], dst_ref=woh.at[:, pl.ds(DL, DL)],
            send_sem=wsem.at[2], recv_sem=wsem.at[3], device_id=CO, device_id_type=MESH,
        ),
    ]
    locals_ = [
        pltpu.make_async_copy(w_in.at[:, ds(core, FH)], wih.at[pl.ds(0, DL), :], lsem.at[0]),
        pltpu.make_async_copy(w_out.at[ds(core, FH), :], woh.at[:, pl.ds(0, DL)], lsem.at[1]),
        pltpu.make_async_copy(w_in, winv, lsem.at[2]),
        pltpu.make_async_copy(w_out, woutv, lsem.at[3]),
    ]
    def near(c, src):
        half = pl.ds(NEAR[c], HT)
        send(xall.at[src, :, half, 0:DL], xall.at[c, :, pl.ds(0, HT), 0:DL], c, AGX, XM)
        send(xall.at[src, :, half, 0:DL], xall.at[c, :, pl.ds(HT, HT), 0:DL], c, AGX, XP)

    def whole(c, src, to):
        send(xall.at[src, :, :, 0:DL], xall.at[c, :, :, 0:DL], c, AGX, to)

    def gather():
        xall[NCH - 1, 0, :, 0:DL] = tok[...]
        xall[NCH - 1, 1, :, 0:DL] = dy[...]
        near(0, NCH - 1)
        whole(2, NCH - 1, ZH)
        whole(1, NCH - 1, XO)

    def forward():
        got(xall.at[2, :, :, 0:DL], 2, AGX)
        near(3, 2)
        whole(4, 2, XO)
        near(5, 2)
        near(6, NCH - 1)

    def s2(c):
        @pl.when((c != 2) & (c != NCH - 1))
        def _():
            got(xall.at[c, :, :, 0:DL], c, AGX)

        send(xall.at[c, :, :, 0:DL], xall.at[c, :, :, DL:DC], c, AGC, CO)
        pl.when(c == 1)(forward)

    def y_rows(d, rows, off):
        return pl.ds(pl.multiple_of(d * rows + off, B), rows)

    def y_send(c, rows, off, c0, h, rel, direct, krel, kdir):
        first, second = pl.ds(c0, h), pl.ds(c0 + h, h)
        send(part.at[c, :, y_rows(yo, rows, off), first], rel.at[c, 0], c, krel, YP)
        send(part.at[c, :, y_rows(yo, rows, off), second], rel.at[c, 1], c, krel, YM)
        send(part.at[c, :, y_rows(yr, rows, off), second], direct.at[c, 0], c, kdir, YP)
        send(part.at[c, :, y_rows(yl, rows, off), first], direct.at[c, 1], c, kdir, YM)

    def y_relay(c, rows, off, c0, h, rel, total, krel, ksum):
        got(rel.at[c], c, krel)
        for i, (d, to) in enumerate(((yr, YP), (yl, YM))):
            place = (c, slice(None), y_rows(d, rows, off), pl.ds(c0 + i * h, h))
            part[place] = (part[place].astype(f32) + rel[c, i].astype(f32)).astype(bf16)
            send(part.at[place], total.at[c, i], c, ksum, to)

    def y_total(c, rows, off, sub, c0, h, direct, total, i):
        own = part[c, :, pl.ds(pl.multiple_of(y * rows + off + sub, B), B), pl.ds(c0 + i * h, h)]
        at = pl.ds(pl.multiple_of(sub, B), B)
        return own.astype(f32) + direct[c, 1 - i, :, at, :].astype(f32) + total[c, i, :, at, :].astype(f32)

    off_b = zl * (4 * B)
    a_mine, b_mine = ds(y * 2 + zl, B), ds(zl * 4 + y, B)

    def s3(c):
        @pl.when(c == 0)
        def _():
            for copy in locals_[:2]:
                copy.wait()
            for copy in swaps:
                copy.wait_recv()

        got(xall.at[c, :, :, DL:DC], c, AGC)

        @pl.loop(0, FH // 256)
        def _(j):
            cols = ds(j, 256)
            part[c, 0, :, cols] = jnp.dot(
                xall[c, 0], wih[:, cols], preferred_element_type=f32
            ).astype(bf16)
            part[c, 1, :, cols] = lax.dot_general(
                xall[c, 1], woh[cols, :], (((1,), (1,)), ((), ())), preferred_element_type=f32
            ).astype(bf16)

        y_send(c, 2 * B, 0, 0, HA, a_rel, a_dir, A_REL, A_DIR)
        send(part.at[c, :, ds(1 - zl, 4 * B), WA:FH], b_z.at[c], c, B_Z, ZL)

    def s4(c):
        y_relay(c, 2 * B, 0, 0, HA, a_rel, a_sum, A_REL, A_SUM)
        got(b_z.at[c], c, B_Z)
        place = (c, slice(None), ds(zl, 4 * B), slice(WA, FH))
        part[place] = (part[place].astype(f32) + b_z[c].astype(f32)).astype(bf16)
        y_send(c, B, off_b, WA, HB, b_rel, b_dir, B_REL, B_DIR)

    def s5(c):
        got(a_dir.at[c], c, A_DIR)
        got(a_sum.at[c], c, A_SUM)
        for i in range(2):
            a_out[c, :, :, i * HA : (i + 1) * HA] = y_total(
                c, 2 * B, 0, (1 - zl) * B, 0, HA, a_dir, a_sum, i
            ).astype(bf16)
        send(a_out.at[c], a_z.at[c], c, A_Z, ZL)
        y_relay(c, B, off_b, WA, HB, b_rel, b_sum, B_REL, B_SUM)

    def unit(c, rows, c0, h, pre, grad):
        half_erf = 0.5 * (1.0 + lax.erf(pre * sqrt_half))
        hid[core, c, 0, rows, c0 : c0 + h] = (pre * half_erf).astype(bf16)
        slope = half_erf + pre * jnp.exp(-0.5 * pre * pre) * inv_root
        hid[core, c, 1, rows, c0 : c0 + h] = (grad * slope).astype(bf16)

    def s6(c):
        got(a_z.at[c], c, A_Z)
        for i in range(2):
            both = y_total(c, 2 * B, 0, zl * B, 0, HA, a_dir, a_sum, i)
            both = both + a_z[c, :, :, i * HA : (i + 1) * HA].astype(f32)
            unit(c, a_mine, i * HA, HA, both[0], both[1])
        view = hid.at[core, c, :, a_mine, 0:WA]
        send(view, view, c, GA_Z, ZL)
        got(b_dir.at[c], c, B_DIR)
        got(b_sum.at[c], c, B_SUM)
        for i in range(2):
            both = y_total(c, B, off_b, 0, WA, HB, b_dir, b_sum, i)
            unit(c, b_mine, WA + i * HB, HB, both[0], both[1])
        view = hid.at[core, c, :, b_mine, WA:FH]
        send(view, view, c, GB_1, YP)
        send(view, view, c, GB_1, YM)

    def y_forward(c, rows, off, c0, h, kind):
        for i, (d, to) in enumerate(((yl, YP), (yr, YM))):
            view = hid.at[core, c, :, y_rows(d, rows, off), pl.ds(c0 + i * h, h)]
            send(view, view, c, kind, to)

    def s7(c):
        got(hid.at[core, c, :, ds(y * 2 + 1 - zl, B), 0:WA], c, GA_Z)
        view = hid.at[core, c, :, ds(y, 2 * B), 0:WA]
        send(view, view, c, GA_1, YP)
        send(view, view, c, GA_1, YM)
        got(hid.at[core, c, :, 0 : 2 * B, WA:FH], c, GB_1)
        y_forward(c, B, off_b, WA, HB, GB_2)

    def s8(c):
        got(hid.at[core, c, :, 0 : 4 * B, 0:WA], c, GA_1)
        y_forward(c, 2 * B, 0, 0, HA, GA_2)
        got(hid.at[core, c, :, 0:B, WA:FH], c, GB_2)
        view = hid.at[core, c, :, ds(zl, 4 * B), WA:FH]
        send(view, view, c, GB_Z, ZL)

    def s9(c):
        got(hid.at[core, c, :, 0 : 2 * B, 0:WA], c, GA_2)
        got(hid.at[core, c, :, 0 : 4 * B, WA:FH], c, GB_Z)
        send(hid.at[core, c], hid.at[core, c], c, GC, CO)

    def s10(c):
        @pl.when(c == 0)
        def _():
            for copy in locals_[2:]:
                copy.wait()

        got(hid.at[other, c], c, GC)
        for k in range(2):
            units = pl.ds(k * FH, FH)
            out = jnp.dot(hid[k, c, 0], woutv[units, :], preferred_element_type=f32)
            back = lax.dot_general(
                hid[k, c, 1], winv[:, units], (((1,), (1,)), ((), ())), preferred_element_type=f32
            )
            if k == 0:
                oc[c, 0], oc[c, 1] = out, back
            else:
                oc[c, 0] += out
                oc[c, 1] += back
        for copy in keep(c):
            copy.start()
        for k, first in NEAR.items():

            @pl.when(c == k)
            def _(k=k, first=first):
                for i, to in enumerate((XP, XM)):
                    dst = xr.at[int(k in (3, 5)), i, :, pl.ds(first, HT), :]
                    send(oc.at[k, :, pl.ds(i * HT, HT), :], dst, k, RX, to)

        for k in FAR:

            @pl.when(c == k)
            def _(k=k):
                send(oc.at[k], xr.at[FAR.index(k), 2], k, RX, XO)

    def keep(c):
        return [
            pltpu.make_async_copy(hid.at[0, c], hid_o.at[0, c], hsem.at[c, 0]),
            pltpu.make_async_copy(hid.at[1, c], hid_o.at[1, c], hsem.at[c, 1]),
            pltpu.make_async_copy(xall.at[c, :, :, 0:DL], xo.at[c], hsem.at[c, 2]),
        ]

    def s11(c):
        for k, chunks, first in ((4, (3, 4), 0), (5, (5,), HT)):

            @pl.when(c == k)
            def _(k=k, chunks=chunks, first=first):
                for chunk in chunks:
                    got(oc.at[chunk], chunk, RX)
                half = pl.ds(first, HT)
                zs[:, half, :] = oc[2, :, half, :] + xr[1, 0, :, half, :] + xr[1, 1, :, half, :] + xr[1, 2, :, half, :]
                send(zs.at[:, half, :], zr.at[:, half, :], k, RZ, ZH)

        @pl.when(c == NCH - 1)
        def _():
            for chunk in (0, 1, 6):
                got(oc.at[chunk], chunk, RX)
            for k in (4, 5):
                got(zr.at[:, 0:HT, :], k, RZ)
            for i, result in enumerate((mlp, ing)):
                total = oc[NCH - 1, i] + xr[0, 0, i] + xr[0, 1, i] + xr[0, 2, i] + zr[i]
                result[...] = total.astype(bf16)

        for copy in keep(c):
            copy.wait()

        @pl.when(c != NCH - 1)
        def _():
            sent(xall.at[c, :, :, 0:DL], c, AGX)

        @pl.when((c != NCH - 1) & (c != 2))
        def _():
            sent(oc.at[c], c, RX)

        @pl.when((c == 4) | (c == 5))
        def _():
            sent(zr.at[:, 0:HT, :], c, RZ)

        sent(xall.at[c, :, :, 0:DL], c, AGC)
        for buf, kind in (
            (a_rel, A_REL), (a_dir, A_DIR), (a_sum, A_SUM), (a_z, A_Z),
            (b_z, B_Z), (b_rel, B_REL), (b_dir, B_DIR), (b_sum, B_SUM),
        ):
            sent(buf.at[c], c, kind)
        for rows, cols, kind in (
            (B, slice(0, WA), GA_Z), (4 * B, slice(0, WA), GA_1), (2 * B, slice(0, WA), GA_2),
            (2 * B, slice(WA, FH), GB_1), (B, slice(WA, FH), GB_2), (4 * B, slice(WA, FH), GB_Z),
        ):
            sent(hid.at[core, c, :, 0:rows, cols], c, kind)
        sent(hid.at[core, c], c, GC)

    gather()
    for copy in locals_:
        copy.start()
    for copy in swaps:
        copy.start()

    order = ((1, s3), (8, s10), (0, s2), (7, s9), (6, s8), (5, s7), (2, s4), (3, s5), (4, s6), (9, s11))

    @pl.loop(0, NCH + STAGES - 1)
    def _(t):
        for stage, work in order:

            @pl.when((t >= stage) & (t < stage + NCH))
            def _(stage=stage, work=work):
                work(t - stage)

    for copy in swaps:
        copy.wait_send()


TILE = 768


def gradients(hid, xo, mlp0, ing0, mlp, ing, wig, wog, xt):
    @pl.when(pl.program_id(0) == 0)
    def _():
        mlp[...] = mlp0[...]
        ing[...] = ing0[...]
        xt[...] = xo[:, 0].reshape(NCH * C, DL).T

    units = hid[0, :, 0].reshape(NCH * C, TILE)
    wog[...] = lax.dot_general(
        units, xo[:, 1].reshape(NCH * C, DL), (((0,), (0,)), ((), ())), preferred_element_type=f32
    )
    wig[...] = jnp.dot(xt[...], hid[0, :, 1].reshape(NCH * C, TILE), preferred_element_type=f32)


def on_device(tokens, w_in, w_out, out_grad):
    vmem, anywhere = pl.BlockSpec(memory_space=pltpu.VMEM), pl.BlockSpec(memory_space=pl.ANY)
    scratch = [
        ((NCH, 2, C, DC), bf16),
        ((DC, FH), bf16),
        ((FH, DC), bf16),
        ((DL, FL), bf16),
        ((FL, DL), bf16),
        ((NCH, 2, C, FH), bf16),
        ((NCH, 2, 2, 2 * B, HA), bf16),
        ((NCH, 2, 2, 2 * B, HA), bf16),
        ((NCH, 2, 2, 2 * B, HA), bf16),
        ((NCH, 2, B, WA), bf16),
        ((NCH, 2, B, WA), bf16),
        ((NCH, 2, 4 * B, WB), bf16),
        ((NCH, 2, 2, B, HB), bf16),
        ((NCH, 2, 2, B, HB), bf16),
        ((NCH, 2, 2, B, HB), bf16),
        ((2, NCH, 2, C, FH), bf16),
        ((NCH, 2, C, DL), f32),
        ((2, 3, 2, TOK, DL), f32),
        ((2, TOK, DL), f32),
        ((2, TOK, DL), f32),
    ]
    mlp, ing, hid, xo = pl.pallas_call(
        kernel,
        out_shape=(
            jax.ShapeDtypeStruct((TOK, DL), bf16),
            jax.ShapeDtypeStruct((TOK, DL), bf16),
            jax.ShapeDtypeStruct((2, NCH, 2, C, FH), bf16),
            jax.ShapeDtypeStruct((NCH, 2, C, DL), bf16),
        ),
        in_specs=[vmem, vmem, anywhere, anywhere],
        out_specs=(vmem, vmem, anywhere, anywhere),
        scratch_shapes=[pltpu.VMEM(shape, dtype) for shape, dtype in scratch]
        + [
            pltpu.SemaphoreType.DMA((NCH, KINDS)),
            pltpu.SemaphoreType.DMA((NCH, KINDS)),
            pltpu.SemaphoreType.DMA((4,)),
            pltpu.SemaphoreType.DMA((4,)),
            pltpu.SemaphoreType.DMA((NCH, 3)),
        ],
        compiler_params=pltpu.CompilerParams(
            collective_id=0, has_side_effects=True, vmem_limit_bytes=62 * 2**20
        ),
    )(tokens, out_grad, w_in, w_out)
    per = FH // TILE
    small = pl.BlockSpec((TOK, DL), lambda j: (0, 0))
    return pl.pallas_call(
        gradients,
        grid=(2 * per,),
        out_shape=(
            jax.ShapeDtypeStruct((TOK, DL), bf16),
            jax.ShapeDtypeStruct((TOK, DL), bf16),
            jax.ShapeDtypeStruct((DL, FL), f32),
            jax.ShapeDtypeStruct((FL, DL), f32),
        ),
        in_specs=[
            pl.BlockSpec((1, NCH, 2, C, TILE), lambda j: (j // per, 0, 0, 0, j % per)),
            pl.BlockSpec((NCH, 2, C, DL), lambda j: (0, 0, 0, 0)),
            small,
            small,
        ],
        out_specs=(
            small,
            small,
            pl.BlockSpec((DL, TILE), lambda j: (0, j)),
            pl.BlockSpec((TILE, DL), lambda j: (j, 0)),
        ),
        scratch_shapes=[pltpu.VMEM((DL, NCH * C), bf16)],
        compiler_params=pltpu.CompilerParams(vmem_limit_bytes=63 * 2**20),
    )(hid, xo, mlp, ing)


def solution(mesh):
    in_specs = (P("row", "col"), P("col", "row"), P("row", "col"), P("row", "col"))
    out_specs = (P("row", "col"), P("row", "col"), P("col", "row"), P("row", "col"))
    return jax.shard_map(
        on_device, mesh=mesh, in_specs=in_specs, out_specs=out_specs, check_vma=False
    )
```

```python
import jax
import jax.numpy as jnp
from jax import lax
from jax.experimental import pallas as pl
from jax.experimental.pallas import tpu as pltpu
from jax.sharding import PartitionSpec as P

MESH = pl.DeviceIdType.MESH
f32, bf16 = jnp.float32, jnp.bfloat16
sqrt_half = 0.7071067811865476
inv_root = 0.3989422804014327

ROWS = 8
TOK = 128
DL = 384
DC = 768
FL = 3072
FH = 1536
NCH = 8
B = TOK // NCH
C = B * ROWS
WA, WB = 896, 640
HA, HB = -(-WA // 256) * 128, -(-WB // 256) * 128
HT = TOK // 2
NEAR = {0: 0, 2: 0, 4: HT, 6: HT}
FAR = (5, 3)
OTHER = 1
STAGES = 11

(AGX, AGC, A_REL, A_DIR, A_SUM, A_Z, B_Z, B_REL, B_DIR, B_SUM, GA_Z, GA_1, GA_2, GB_1, GB_2, GB_Z, GC_A, GC_B, RX, RZ) = range(20)
KINDS = 20


def kernel(
    tok, dy, w_in, w_out,
    mlp, ing, hidt_o, pg_o, xt_o, dy_o,
    xall, wih, woh, winv, woutv, part,
    a_rel, a_dir, a_sum, a_out, a_z, b_z, b_rel, b_dir, b_sum,
    hid, hidt, xt, oc, xr, zs, zr,
    ssem, rsem, wsem, lsem, hsem,
):
    row, col = lax.axis_index("row"), lax.axis_index("col")
    x, zh = row // 2, row % 2
    zl, y, core = col // 8, (col // 2) % 4, col % 2
    other = 1 - core

    def dev(dx=0, dzh=0, dzl=0, dyy=0, dc=0):
        return (
            ((x + dx) % 4) * 2 + (zh + dzh) % 2,
            (((zl + dzl) % 2) * 4 + (y + dyy) % 4) * 2 + (core + dc) % 2,
        )

    XP, XM, XO = dev(dx=1), dev(dx=3), dev(dx=2)
    ZH, ZL = dev(dzh=1), dev(dzl=1)
    YP, YM = dev(dyy=1), dev(dyy=3)
    CO = dev(dc=1)
    yr, yl, yo = (y + 1) % 4, (y + 3) % 4, (y + 2) % 4

    def send(src, dst, c, kind, to):
        pltpu.make_async_remote_copy(
            src_ref=src, dst_ref=dst, send_sem=ssem.at[c, kind], recv_sem=rsem.at[c, kind],
            device_id=to, device_id_type=MESH,
        ).start()

    def got(view, c, kind):
        pltpu.make_async_copy(view, view, rsem.at[c, kind]).wait()

    def sent(view, c, kind):
        pltpu.make_async_copy(view, view, ssem.at[c, kind]).wait()

    def ds(i, size):
        return pl.ds(pl.multiple_of(i * size, size), size)

    barrier = pltpu.get_barrier_semaphore()
    for d in (XP, XM, XO, ZH, ZL, YP, YM, CO):
        pl.semaphore_signal(barrier, 1, device_id=d, device_id_type=MESH)
    takes = [
        pltpu.make_async_copy(src, xall.at[NCH - 1, i, :, 0:DL], lsem.at[4 + i]) for i, src in enumerate((tok, dy))
    ]
    for copy in takes:
        copy.start()
    pl.semaphore_wait(barrier, 8)

    swaps = [
        pltpu.make_async_remote_copy(
            src_ref=w_in.at[:, ds(other, FH)], dst_ref=wih.at[pl.ds(DL, DL), :],
            send_sem=wsem.at[0], recv_sem=wsem.at[1], device_id=CO, device_id_type=MESH,
        ),
        pltpu.make_async_remote_copy(
            src_ref=w_out.at[ds(other, FH), :], dst_ref=woh.at[:, pl.ds(DL, DL)],
            send_sem=wsem.at[2], recv_sem=wsem.at[3], device_id=CO, device_id_type=MESH,
        ),
    ]
    locals_ = [
        pltpu.make_async_copy(w_in.at[:, ds(core, FH)], wih.at[pl.ds(0, DL), :], lsem.at[0]),
        pltpu.make_async_copy(w_out.at[ds(core, FH), :], woh.at[:, pl.ds(0, DL)], lsem.at[1]),
        pltpu.make_async_copy(w_in, winv, lsem.at[2]),
        pltpu.make_async_copy(w_out, woutv, lsem.at[3]),
    ]
    def near(c, src):
        half = pl.ds(NEAR[c], HT)
        send(xall.at[src, :, half, 0:DL], xall.at[c, :, pl.ds(0, HT), 0:DL], c, AGX, XM)
        send(xall.at[src, :, half, 0:DL], xall.at[c, :, pl.ds(HT, HT), 0:DL], c, AGX, XP)

    def whole(c, src, to):
        send(xall.at[src, :, :, 0:DL], xall.at[c, :, :, 0:DL], c, AGX, to)

    def gather():
        near(0, NCH - 1)
        whole(OTHER, NCH - 1, ZH)

    def forward():
        got(xall.at[OTHER, :, :, 0:DL], OTHER, AGX)
        near(2, OTHER)
        whole(FAR[1], OTHER, XO)
        near(4, OTHER)
        whole(FAR[0], NCH - 1, XO)
        near(6, NCH - 1)

    def s2(c):
        pl.when(c == OTHER)(forward)

        @pl.when((c != OTHER) & (c != NCH - 1))
        def _():
            got(xall.at[c, :, :, 0:DL], c, AGX)

        send(xall.at[c, :, :, 0:DL], xall.at[c, :, :, DL:DC], c, AGC, CO)

    def y_rows(d, rows, off):
        return pl.ds(pl.multiple_of(d * rows + off, B), rows)

    def y_send(c, rows, off, c0, cut, c1, rel, direct, krel, kdir):
        h = cut - c0
        for i, (half, place) in enumerate(((pl.ds(c0, h), pl.ds(0, h)), (pl.ds(cut, c1 - cut), pl.ds(h, c1 - cut)))):
            send(part.at[c, :, y_rows(yo, rows, off), half], rel.at[c, :, :, place], c, krel, (YP, YM)[i])
            d, to = ((yl, YM), (yr, YP))[i]
            send(part.at[c, :, y_rows(d, rows, off), half], direct.at[c, :, :, place], c, kdir, to)

    def y_relay(c, rows, off, c0, cut, c1, rel, total, krel, ksum):
        got(rel.at[c], c, krel)
        h = cut - c0
        for half, at, d, to in (
            (pl.ds(c0, h), pl.ds(0, h), yr, YP), (pl.ds(cut, c1 - cut), pl.ds(h, c1 - cut), yl, YM),
        ):
            place = (c, slice(None), y_rows(d, rows, off), half)
            part[place] = (part[place].astype(f32) + rel[c, :, :, at].astype(f32)).astype(bf16)
            send(part.at[place], total.at[c, :, :, at], c, ksum, to)

    def y_total(c, rows, off, sub, c0, c1, direct, total):
        own = part[c, :, pl.ds(pl.multiple_of(y * rows + off + sub, B), B), c0:c1]
        at = pl.ds(pl.multiple_of(sub, B), B)
        return own.astype(f32) + direct[c, :, at, :].astype(f32) + total[c, :, at, :].astype(f32)

    off_b = zl * (4 * B)
    route_a = (2 * B, 0, 0, HA, WA)
    route_b = (B, off_b, WA, WA + HB, FH)
    a_mine, b_mine = ds(y * 2 + zl, B), ds(zl * 4 + y, B)

    def s3(c):
        @pl.when(c == 0)
        def _():
            for copy in locals_[:2]:
                copy.wait()
            for copy in swaps:
                copy.wait_recv()

        got(xall.at[c, :, :, DL:DC], c, AGC)

        def products(first, end):
            @pl.loop(first, end)
            def _(j):
                cols = ds(j, 256)
                part[c, 0, :, cols] = jnp.dot(
                    xall[c, 0], wih[:, cols], preferred_element_type=f32
                ).astype(bf16)
                part[c, 1, :, cols] = lax.dot_general(
                    xall[c, 1], woh[cols, :], (((1,), (1,)), ((), ())), preferred_element_type=f32
                ).astype(bf16)

        products(0, -(-WA // 256))
        y_send(c, *route_a, a_rel, a_dir, A_REL, A_DIR)
        products(-(-WA // 256), FH // 256)
        send(part.at[c, :, ds(1 - zl, 4 * B), WA:FH], b_z.at[c], c, B_Z, ZL)

    def s4a(c):
        y_relay(c, *route_a, a_rel, a_sum, A_REL, A_SUM)

    def s4b(c):
        got(b_z.at[c], c, B_Z)
        place = (c, slice(None), ds(zl, 4 * B), slice(WA, FH))
        part[place] = (part[place].astype(f32) + b_z[c].astype(f32)).astype(bf16)
        y_send(c, *route_b, b_rel, b_dir, B_REL, B_DIR)

    def s5a(c):
        got(a_dir.at[c], c, A_DIR)
        got(a_sum.at[c], c, A_SUM)
        a_out[c] = y_total(c, 2 * B, 0, (1 - zl) * B, 0, WA, a_dir, a_sum).astype(bf16)
        send(a_out.at[c], a_z.at[c], c, A_Z, ZL)

    def s5b(c):
        y_relay(c, *route_b, b_rel, b_sum, B_REL, B_SUM)

    def unit(c, rows, c0, c1, both):
        pre, grad = both[0], both[1]
        half_erf = 0.5 * (1.0 + lax.erf(pre * sqrt_half))
        hid[core, c, 0, rows, c0:c1] = (pre * half_erf).astype(bf16)
        slope = half_erf + pre * jnp.exp(-0.5 * pre * pre) * inv_root
        hid[core, c, 1, rows, c0:c1] = (grad * slope).astype(bf16)

    def s6a(c):
        got(a_z.at[c], c, A_Z)
        unit(c, a_mine, 0, WA, y_total(c, 2 * B, 0, zl * B, 0, WA, a_dir, a_sum) + a_z[c].astype(f32))
        view = hid.at[core, c, :, a_mine, 0:WA]
        send(view, view, c, GA_Z, ZL)

    def s6b(c):
        got(b_dir.at[c], c, B_DIR)
        got(b_sum.at[c], c, B_SUM)
        unit(c, b_mine, WA, FH, y_total(c, B, off_b, 0, WA, FH, b_dir, b_sum))
        view = hid.at[core, c, :, b_mine, WA:FH]
        send(view, view, c, GB_1, YP)
        send(view, view, c, GB_1, YM)

    def y_forward(c, rows, off, c0, cut, c1, kind):
        for d, half, to in ((yl, pl.ds(c0, cut - c0), YP), (yr, pl.ds(cut, c1 - cut), YM)):
            view = hid.at[core, c, :, y_rows(d, rows, off), half]
            send(view, view, c, kind, to)

    def s7a(c):
        got(hid.at[core, c, :, ds(y * 2 + 1 - zl, B), 0:WA], c, GA_Z)
        view = hid.at[core, c, :, ds(y, 2 * B), 0:WA]
        send(view, view, c, GA_1, YP)
        send(view, view, c, GA_1, YM)

    def s7b(c):
        got(hid.at[core, c, :, 0 : 2 * B, WA:FH], c, GB_1)
        y_forward(c, *route_b, GB_2)

    def s8a(c):
        got(hid.at[core, c, :, 0 : 4 * B, 0:WA], c, GA_1)
        y_forward(c, *route_a, GA_2)

    def s8b(c):
        got(hid.at[core, c, :, 0:B, WA:FH], c, GB_2)
        view = hid.at[core, c, :, ds(zl, 4 * B), WA:FH]
        send(view, view, c, GB_Z, ZL)

    def s9a(c):
        got(hid.at[core, c, :, 0 : 2 * B, 0:WA], c, GA_2)
        send(hid.at[core, c, :, :, 0:WA], hid.at[core, c, :, :, 0:WA], c, GC_A, CO)

    def s9b(c):
        got(hid.at[core, c, :, 0 : 4 * B, WA:FH], c, GB_Z)
        send(hid.at[core, c, :, :, WA:FH], hid.at[core, c, :, :, WA:FH], c, GC_B, CO)

    def s10(c):
        @pl.when(c == 0)
        def _():
            for copy in locals_[2:]:
                copy.wait()

        got(hid.at[other, c, :, :, 0:WA], c, GC_A)
        got(hid.at[other, c, :, :, WA:FH], c, GC_B)
        for k in range(2):
            units = pl.ds(k * FH, FH)
            out = jnp.dot(hid[k, c, 0], woutv[units, :], preferred_element_type=f32)
            back = lax.dot_general(
                hid[k, c, 1], winv[:, units], (((1,), (1,)), ((), ())), preferred_element_type=f32
            )
            if k == 0:
                oc[c, 0], oc[c, 1] = out, back
            else:
                oc[c, 0] += out
                oc[c, 1] += back
        for k, first in NEAR.items():

            @pl.when(c == k)
            def _(k=k, first=first):
                for i, to in enumerate((XP, XM)):
                    dst = xr.at[int(k in (2, 4)), i, :, pl.ds(first, HT), :]
                    send(oc.at[k, :, pl.ds(i * HT, HT), :], dst, k, RX, to)

        for k in FAR:

            @pl.when(c == k)
            def _(k=k):
                send(oc.at[k], xr.at[FAR.index(k), 2], k, RX, XO)

        @pl.when(c >= 2)
        def _():
            for copy in keep(c - 2):
                copy.wait()

        for k in range(2):
            hidt[c % 2, k * FH : (k + 1) * FH, :] = hid[k, c, 0].T
        xt[c % 2] = xall[c, 0, :, 0:DL].T
        for copy in keep(c):
            copy.start()

    def keep(c):
        tokens = ds(c, C)
        copies = [
            (hidt.at[c % 2], hidt_o.at[:, tokens]),
            (hid.at[0, c, 1], pg_o.at[tokens, 0:FH]),
            (hid.at[1, c, 1], pg_o.at[tokens, FH:FL]),
            (xt.at[c % 2], xt_o.at[:, tokens]),
            (xall.at[c, 1, :, 0:DL], dy_o.at[tokens, :]),
        ]
        return [pltpu.make_async_copy(*pair, hsem.at[c, i]) for i, pair in enumerate(copies)]

    def s11(c):
        for k, chunks, first in ((4, (2, 3), 0), (5, (4,), HT)):

            @pl.when(c == k)
            def _(k=k, chunks=chunks, first=first):
                for chunk in chunks:
                    got(oc.at[chunk], chunk, RX)
                half = pl.ds(first, HT)
                zs[:, half, :] = oc[OTHER, :, half, :] + xr[1, 0, :, half, :] + xr[1, 1, :, half, :] + xr[1, 2, :, half, :]
                send(zs.at[:, half, :], zr.at[:, half, :], k, RZ, ZH)

        @pl.when(c == NCH - 1)
        def _():
            for chunk in (0, 5, 6):
                got(oc.at[chunk], chunk, RX)
            for k in (4, 5):
                got(zr.at[:, 0:HT, :], k, RZ)
            for i, result in enumerate((mlp, ing)):
                total = oc[NCH - 1, i] + xr[0, 0, i] + xr[0, 1, i] + xr[0, 2, i] + zr[i]
                result[...] = total.astype(bf16)

    def s12(c):
        @pl.when(c >= NCH - 2)
        def _():
            for copy in keep(c):
                copy.wait()

        @pl.when(c != NCH - 1)
        def _():
            sent(xall.at[c, :, :, 0:DL], c, AGX)

        @pl.when((c != NCH - 1) & (c != OTHER))
        def _():
            sent(oc.at[c], c, RX)

        @pl.when((c == 4) | (c == 5))
        def _():
            sent(zr.at[:, 0:HT, :], c, RZ)

        sent(xall.at[c, :, :, 0:DL], c, AGC)
        for buf, kind in (
            (a_rel, A_REL), (a_dir, A_DIR), (a_sum, A_SUM), (a_z, A_Z),
            (b_z, B_Z), (b_rel, B_REL), (b_dir, B_DIR), (b_sum, B_SUM),
        ):
            sent(buf.at[c], c, kind)
        for rows, cols, kind in (
            (B, slice(0, WA), GA_Z), (4 * B, slice(0, WA), GA_1), (2 * B, slice(0, WA), GA_2),
            (2 * B, slice(WA, FH), GB_1), (B, slice(WA, FH), GB_2), (4 * B, slice(WA, FH), GB_Z),
        ):
            sent(hid.at[core, c, :, 0:rows, cols], c, kind)
        sent(hid.at[core, c, :, :, 0:WA], c, GC_A)
        sent(hid.at[core, c, :, :, WA:FH], c, GC_B)

    for copy in takes:
        copy.wait()
    gather()
    for copy in locals_:
        copy.start()
    for copy in swaps:
        copy.start()

    order = (
        (1, s3), (8, s10), (0, s2), (7, s9a), (7, s9b), (6, s8a), (6, s8b), (5, s7a),
        (5, s7b), (2, s4a), (2, s4b), (3, s5a), (3, s5b), (4, s6a), (4, s6b), (9, s11),
        (10, s12),
    )

    @pl.loop(0, NCH + STAGES - 1)
    def _(t):
        for stage, work in order:

            @pl.when((t >= stage) & (t < stage + NCH))
            def _(stage=stage, work=work):
                work(t - stage)

    for copy in swaps:
        copy.wait_send()


TILE = 768


def gradients(hidt, pg, xt, dy, mlp0, ing0, mlp, ing, wig, wog, gi, go, sem):
    copies = [
        pltpu.make_async_copy(mlp0, mlp, sem.at[0, 0]),
        pltpu.make_async_copy(ing0, ing, sem.at[1, 0]),
    ]
    for copy in copies:
        copy.start()
    for j in range(FL // TILE):
        units = pl.ds(j * TILE, TILE)
        go[units, :] = jnp.dot(hidt[units, :], dy[...], preferred_element_type=f32)
        gi[:, units] = jnp.dot(xt[...], pg[:, units], preferred_element_type=f32)
        for copy in (
            pltpu.make_async_copy(go.at[units, :], wog.at[units, :], sem.at[0, j + 1]),
            pltpu.make_async_copy(gi.at[:, units], wig.at[:, units], sem.at[1, j + 1]),
        ):
            copy.start()
            copies.append(copy)
    for copy in copies:
        copy.wait()


def on_device(tokens, w_in, w_out, out_grad):
    vmem, anywhere = pl.BlockSpec(memory_space=pltpu.VMEM), pl.BlockSpec(memory_space=pl.ANY)
    scratch = [
        ((NCH, 2, C, DC), bf16),
        ((DC, FH), bf16),
        ((FH, DC), bf16),
        ((DL, FL), bf16),
        ((FL, DL), bf16),
        ((NCH, 2, C, FH), bf16),
        ((NCH, 2, 2 * B, WA), bf16),
        ((NCH, 2, 2 * B, WA), bf16),
        ((NCH, 2, 2 * B, WA), bf16),
        ((NCH, 2, B, WA), bf16),
        ((NCH, 2, B, WA), bf16),
        ((NCH, 2, 4 * B, WB), bf16),
        ((NCH, 2, B, WB), bf16),
        ((NCH, 2, B, WB), bf16),
        ((NCH, 2, B, WB), bf16),
        ((2, NCH, 2, C, FH), bf16),
        ((2, FL, C), bf16),
        ((2, DL, C), bf16),
        ((NCH, 2, C, DL), f32),
        ((2, 3, 2, TOK, DL), f32),
        ((2, TOK, DL), f32),
        ((2, TOK, DL), f32),
    ]
    mlp, ing, hidt, pg, xt, dy = pl.pallas_call(
        kernel,
        out_shape=(
            pltpu.VMEM((TOK, DL), bf16),
            pltpu.VMEM((TOK, DL), bf16),
            pltpu.VMEM((FL, NCH * C), bf16),
            pltpu.VMEM((NCH * C, FL), bf16),
            pltpu.VMEM((DL, NCH * C), bf16),
            pltpu.VMEM((NCH * C, DL), bf16),
        ),
        in_specs=[anywhere] * 4,
        out_specs=(vmem, vmem, anywhere, anywhere, anywhere, anywhere),
        scratch_shapes=[pltpu.VMEM(shape, dtype) for shape, dtype in scratch]
        + [
            pltpu.SemaphoreType.DMA((NCH, KINDS)),
            pltpu.SemaphoreType.DMA((NCH, KINDS)),
            pltpu.SemaphoreType.DMA((4,)),
            pltpu.SemaphoreType.DMA((6,)),
            pltpu.SemaphoreType.DMA((NCH, 5)),
        ],
        compiler_params=pltpu.CompilerParams(
            collective_id=0, has_side_effects=True, vmem_limit_bytes=46 * 2**20
        ),
    )(tokens, out_grad, w_in, w_out)
    mlp, ing, hidt, pg, xt, dy = (
        pltpu.with_memory_space_constraint(v, pltpu.VMEM) for v in (mlp, ing, hidt, pg, xt, dy)
    )
    return pl.pallas_call(
        gradients,
        out_shape=(
            jax.ShapeDtypeStruct((TOK, DL), bf16),
            jax.ShapeDtypeStruct((TOK, DL), bf16),
            jax.ShapeDtypeStruct((DL, FL), f32),
            jax.ShapeDtypeStruct((FL, DL), f32),
        ),
        in_specs=[vmem] * 6,
        out_specs=(anywhere,) * 4,
        scratch_shapes=[
            pltpu.VMEM((DL, FL), f32),
            pltpu.VMEM((FL, DL), f32),
            pltpu.SemaphoreType.DMA((2, FL // TILE + 1)),
        ],
        compiler_params=pltpu.CompilerParams(vmem_limit_bytes=24 * 2**20),
    )(hidt, pg, xt, dy, mlp, ing)


def solution(mesh):
    in_specs = (P("row", "col"), P("col", "row"), P("row", "col"), P("row", "col"))
    out_specs = (P("row", "col"), P("row", "col"), P("col", "row"), P("row", "col"))
    return jax.shard_map(
        on_device, mesh=mesh, in_specs=in_specs, out_specs=out_specs, check_vma=False
    )
```

```python
import jax
import jax.numpy as jnp
from jax import lax
from jax.experimental import pallas as pl
from jax.experimental.pallas import tpu as pltpu
from jax.sharding import PartitionSpec as P

MESH = pl.DeviceIdType.MESH
f32, bf16 = jnp.float32, jnp.bfloat16
sqrt_half = 0.7071067811865476
inv_root = 0.3989422804014327

ROWS = 8
TOK = 128
DL = 384
DC = 768
FL = 3072
FH = 1536
NCH = 8
B = TOK // NCH
C = B * ROWS
WA, WB = 1024, 512
HA, HB = -(-WA // 256) * 128, -(-WB // 256) * 128
HT = TOK // 2
NEAR = {0: 0, 2: 0, 4: HT, 6: HT}
FAR = (5, 3)
OTHER = 1
STAGES = 11
FIRST, LAST = 12, 16
HALF = NCH // 2 * C

(AGX, AGC, A_REL, A_DIR, A_SUM, A_Z, B_Z, B_REL, B_DIR, B_SUM, GA_Z, GA_1, GA_2, GB_1, GB_2, GB_Z, GC_A, GC_B, RX, RZ) = range(20)
KINDS = 20


def kernel(
    tok, dy, w_in, w_out,
    mlp, ing, xt, down, hidt, grads, p_in, p_out,
    xall, wih, woh, winv, woutv, part,
    a_rel, a_dir, a_sum, a_out, a_z, b_z, b_rel, b_dir, b_sum,
    hid, oc, xr, near6, xr6, zs, zr,
    ssem, rsem, wsem, lsem,
):
    row, col = lax.axis_index("row"), lax.axis_index("col")
    x, zh = row // 2, row % 2
    zl, y, core = col // 8, (col // 2) % 4, col % 2
    other = 1 - core

    def dev(dx=0, dzh=0, dzl=0, dyy=0, dc=0):
        return (
            ((x + dx) % 4) * 2 + (zh + dzh) % 2,
            (((zl + dzl) % 2) * 4 + (y + dyy) % 4) * 2 + (core + dc) % 2,
        )

    XP, XM, XO = dev(dx=1), dev(dx=3), dev(dx=2)
    ZH, ZL = dev(dzh=1), dev(dzl=1)
    YP, YM = dev(dyy=1), dev(dyy=3)
    CO = dev(dc=1)
    yr, yl, yo = (y + 1) % 4, (y + 3) % 4, (y + 2) % 4

    def send(src, dst, c, kind, to):
        pltpu.make_async_remote_copy(
            src_ref=src, dst_ref=dst, send_sem=ssem.at[c, kind], recv_sem=rsem.at[c, kind],
            device_id=to, device_id_type=MESH,
        ).start()

    def got(view, c, kind):
        pltpu.make_async_copy(view, view, rsem.at[c, kind]).wait()

    def sent(view, c, kind):
        pltpu.make_async_copy(view, view, ssem.at[c, kind]).wait()

    def ds(i, size):
        return pl.ds(pl.multiple_of(i * size, size), size)

    barrier = pltpu.get_barrier_semaphore()
    for d in (XP, XM, XO, ZH, ZL, YP, YM, CO):
        pl.semaphore_signal(barrier, 1, device_id=d, device_id_type=MESH)
    takes = [
        pltpu.make_async_copy(src, xall.at[NCH - 1, i, :, 0:DL], lsem.at[4 + i]) for i, src in enumerate((tok, dy))
    ]
    for copy in takes:
        copy.start()
    pl.semaphore_wait(barrier, 8)

    swaps = [
        pltpu.make_async_remote_copy(
            src_ref=w_in.at[:, ds(other, FH)], dst_ref=wih.at[pl.ds(DL, DL), :],
            send_sem=wsem.at[0], recv_sem=wsem.at[1], device_id=CO, device_id_type=MESH,
        ),
        pltpu.make_async_remote_copy(
            src_ref=w_out.at[ds(other, FH), :], dst_ref=woh.at[:, pl.ds(DL, DL)],
            send_sem=wsem.at[2], recv_sem=wsem.at[3], device_id=CO, device_id_type=MESH,
        ),
    ]
    locals_ = [
        pltpu.make_async_copy(w_in.at[:, ds(core, FH)], wih.at[pl.ds(0, DL), :], lsem.at[0]),
        pltpu.make_async_copy(w_out.at[ds(core, FH), :], woh.at[:, pl.ds(0, DL)], lsem.at[1]),
        pltpu.make_async_copy(w_in, winv, lsem.at[2]),
        pltpu.make_async_copy(w_out, woutv, lsem.at[3]),
    ]
    def near(c, src):
        half = pl.ds(NEAR[c], HT)
        send(xall.at[src, :, half, 0:DL], xall.at[c, :, pl.ds(0, HT), 0:DL], c, AGX, XM)
        send(xall.at[src, :, half, 0:DL], xall.at[c, :, pl.ds(HT, HT), 0:DL], c, AGX, XP)

    def whole(c, src, to):
        send(xall.at[src, :, :, 0:DL], xall.at[c, :, :, 0:DL], c, AGX, to)

    def gather():
        near(0, NCH - 1)
        whole(OTHER, NCH - 1, ZH)

    def forward():
        got(xall.at[OTHER, :, :, 0:DL], OTHER, AGX)
        near(2, OTHER)
        whole(FAR[1], OTHER, XO)
        near(4, OTHER)
        whole(FAR[0], NCH - 1, XO)
        near(6, NCH - 1)

    def s2(c):
        pl.when(c == OTHER)(forward)

        @pl.when((c != OTHER) & (c != NCH - 1))
        def _():
            got(xall.at[c, :, :, 0:DL], c, AGX)

        send(xall.at[c, :, :, 0:DL], xall.at[c, :, :, DL:DC], c, AGC, CO)

    def y_rows(d, rows, off):
        return pl.ds(pl.multiple_of(d * rows + off, B), rows)

    def y_send(c, rows, off, c0, cut, c1, rel, direct, krel, kdir):
        h = cut - c0
        for i, (half, place) in enumerate(((pl.ds(c0, h), pl.ds(0, h)), (pl.ds(cut, c1 - cut), pl.ds(h, c1 - cut)))):
            send(part.at[c, :, y_rows(yo, rows, off), half], rel.at[c, :, :, place], c, krel, (YP, YM)[i])
            d, to = ((yl, YM), (yr, YP))[i]
            send(part.at[c, :, y_rows(d, rows, off), half], direct.at[c, :, :, place], c, kdir, to)

    def y_relay(c, rows, off, c0, cut, c1, rel, total, krel, ksum):
        got(rel.at[c], c, krel)
        h = cut - c0
        for half, at, d, to in (
            (pl.ds(c0, h), pl.ds(0, h), yr, YP), (pl.ds(cut, c1 - cut), pl.ds(h, c1 - cut), yl, YM),
        ):
            place = (c, slice(None), y_rows(d, rows, off), half)
            part[place] = (part[place].astype(f32) + rel[c, :, :, at].astype(f32)).astype(bf16)
            send(part.at[place], total.at[c, :, :, at], c, ksum, to)

    def y_total(c, rows, off, sub, c0, c1, direct, total):
        own = part[c, :, pl.ds(pl.multiple_of(y * rows + off + sub, B), B), c0:c1]
        at = pl.ds(pl.multiple_of(sub, B), B)
        return own.astype(f32) + direct[c, :, at, :].astype(f32) + total[c, :, at, :].astype(f32)

    off_b = zl * (4 * B)
    route_a = (2 * B, 0, 0, HA, WA)
    route_b = (B, off_b, WA, WA + HB, FH)
    a_mine, b_mine = ds(y * 2 + zl, B), ds(zl * 4 + y, B)

    def s3(c):
        @pl.when(c == 0)
        def _():
            for copy in locals_[:2]:
                copy.wait()
            for copy in swaps:
                copy.wait_recv()

        got(xall.at[c, :, :, DL:DC], c, AGC)

        def products(first, end):
            @pl.loop(first, end)
            def _(j):
                cols = ds(j, 256)
                part[c, 0, :, cols] = jnp.dot(
                    xall[c, 0], wih[:, cols], preferred_element_type=f32
                ).astype(bf16)
                part[c, 1, :, cols] = lax.dot_general(
                    xall[c, 1], woh[cols, :], (((1,), (1,)), ((), ())), preferred_element_type=f32
                ).astype(bf16)

        products(0, -(-WA // 256))
        y_send(c, *route_a, a_rel, a_dir, A_REL, A_DIR)
        products(-(-WA // 256), FH // 256)
        send(part.at[c, :, ds(1 - zl, 4 * B), WA:FH], b_z.at[c], c, B_Z, ZL)

    def s4a(c):
        y_relay(c, *route_a, a_rel, a_sum, A_REL, A_SUM)

    def s4b(c):
        got(b_z.at[c], c, B_Z)
        place = (c, slice(None), ds(zl, 4 * B), slice(WA, FH))
        part[place] = (part[place].astype(f32) + b_z[c].astype(f32)).astype(bf16)
        y_send(c, *route_b, b_rel, b_dir, B_REL, B_DIR)

    def s5a(c):
        got(a_dir.at[c], c, A_DIR)
        got(a_sum.at[c], c, A_SUM)
        a_out[c] = y_total(c, 2 * B, 0, (1 - zl) * B, 0, WA, a_dir, a_sum).astype(bf16)
        send(a_out.at[c], a_z.at[c], c, A_Z, ZL)

    def s5b(c):
        y_relay(c, *route_b, b_rel, b_sum, B_REL, B_SUM)

    def unit(c, rows, c0, c1, both):
        pre, grad = both[0], both[1]
        half_erf = 0.5 * (1.0 + lax.erf(pre * sqrt_half))
        hid[core, c, 0, rows, c0:c1] = (pre * half_erf).astype(bf16)
        slope = half_erf + pre * jnp.exp(-0.5 * pre * pre) * inv_root
        hid[core, c, 1, rows, c0:c1] = (grad * slope).astype(bf16)

    def s6a(c):
        got(a_z.at[c], c, A_Z)
        unit(c, a_mine, 0, WA, y_total(c, 2 * B, 0, zl * B, 0, WA, a_dir, a_sum) + a_z[c].astype(f32))
        view = hid.at[core, c, :, a_mine, 0:WA]
        send(view, view, c, GA_Z, ZL)

    def s6b(c):
        got(b_dir.at[c], c, B_DIR)
        got(b_sum.at[c], c, B_SUM)
        unit(c, b_mine, WA, FH, y_total(c, B, off_b, 0, WA, FH, b_dir, b_sum))
        view = hid.at[core, c, :, b_mine, WA:FH]
        send(view, view, c, GB_1, YP)
        send(view, view, c, GB_1, YM)

    def y_forward(c, rows, off, c0, cut, c1, kind):
        for d, half, to in ((yl, pl.ds(c0, cut - c0), YP), (yr, pl.ds(cut, c1 - cut), YM)):
            view = hid.at[core, c, :, y_rows(d, rows, off), half]
            send(view, view, c, kind, to)

    def s7a(c):
        got(hid.at[core, c, :, ds(y * 2 + 1 - zl, B), 0:WA], c, GA_Z)
        view = hid.at[core, c, :, ds(y, 2 * B), 0:WA]
        send(view, view, c, GA_1, YP)
        send(view, view, c, GA_1, YM)

    def s7b(c):
        got(hid.at[core, c, :, 0 : 2 * B, WA:FH], c, GB_1)
        y_forward(c, *route_b, GB_2)

    def s8a(c):
        got(hid.at[core, c, :, 0 : 4 * B, 0:WA], c, GA_1)
        y_forward(c, *route_a, GA_2)

    def s8b(c):
        got(hid.at[core, c, :, 0:B, WA:FH], c, GB_2)
        view = hid.at[core, c, :, ds(zl, 4 * B), WA:FH]
        send(view, view, c, GB_Z, ZL)

    def s9a(c):
        got(hid.at[core, c, :, 0 : 2 * B, 0:WA], c, GA_2)
        send(hid.at[core, c, :, :, 0:WA], hid.at[core, c, :, :, 0:WA], c, GC_A, CO)

    def s9b(c):
        got(hid.at[core, c, :, 0 : 4 * B, WA:FH], c, GB_Z)
        send(hid.at[core, c, :, :, WA:FH], hid.at[core, c, :, :, WA:FH], c, GC_B, CO)

    def s10(c):
        @pl.when(c == 0)
        def _():
            for copy in locals_[2:]:
                copy.wait()

        def products(half):
            units = ds(half, FH)
            out = jnp.dot(hid[half, c, 0], woutv[units, :], preferred_element_type=f32)
            back = lax.dot_general(
                hid[half, c, 1], winv[:, units], (((1,), (1,)), ((), ())), preferred_element_type=f32
            )
            return out, back

        oc[c, 0], oc[c, 1] = products(core)
        got(hid.at[other, c, :, :, 0:WA], c, GC_A)
        got(hid.at[other, c, :, :, WA:FH], c, GC_B)
        out, back = products(other)
        oc[c, 0] += out
        oc[c, 1] += back
        for k, first in NEAR.items():
            if k == 6:
                continue

            @pl.when(c == k)
            def _(k=k, first=first):
                for i, to in enumerate((XP, XM)):
                    dst = xr.at[int(k in (2, 4)), i, :, pl.ds(first, HT), :]
                    send(oc.at[k, :, pl.ds(i * HT, HT), :], dst, k, RX, to)

        @pl.when(c == 6)
        def _():
            near6[...] = oc[6].astype(bf16)
            for i, to in enumerate((XP, XM)):
                send(near6.at[:, pl.ds(i * HT, HT), :], xr6.at[i], 6, RX, to)

        for k in FAR:

            @pl.when(c == k)
            def _(k=k):
                send(oc.at[k], xr.at[FAR.index(k), 2], k, RX, XO)

        @pl.when(c >= NCH // 2)
        def _():
            tokens = ds(c - NCH // 2, C)
            for k in range(2):
                hidt[k * FH : (k + 1) * FH, tokens] = hid[k, c, 0].T
                grads[tokens, k * FH : (k + 1) * FH] = hid[k, c, 1]
            xt[:, tokens] = xall[c, 0, :, 0:DL].T
            down[tokens, :] = xall[c, 1, :, 0:DL]

    def early(t):
        tiles = FL // 256 // (LAST - FIRST)
        first = pl.ds(0, NCH // 2)
        tn = (((0,), (0,)), ((), ()))
        up_t = xall[first, 0, :, 0:DL].reshape(HALF, DL).T

        @pl.loop(0, tiles)
        def _(i):
            j = (t - FIRST) * tiles + i
            units, k, place = ds(j, 256), j // 6, ds(j % 6, 256)
            p_out[units, :] = lax.dot_general(
                hid[k, first, 0, :, place].reshape(HALF, 256),
                xall[first, 1, :, 0:DL].reshape(HALF, DL),
                tn,
                preferred_element_type=f32,
            )
            p_in[:, units] = jnp.dot(
                up_t, hid[k, first, 1, :, place].reshape(HALF, 256), preferred_element_type=f32
            )

    def s11(c):
        for k, chunks, first in ((4, (2, 3), 0), (5, (4,), HT)):

            @pl.when(c == k)
            def _(k=k, chunks=chunks, first=first):
                for chunk in chunks:
                    got(oc.at[chunk], chunk, RX)
                half = pl.ds(first, HT)
                total = oc[OTHER, :, half, :] + xr[1, 2, :, half, :]
                zs[:, half, :] = (total + xr[1, 0, :, half, :] + xr[1, 1, :, half, :]).astype(bf16)
                send(zs.at[:, half, :], zr.at[:, half, :], k, RZ, ZH)

        @pl.when(c == NCH - 1)
        def _():
            for chunk in (0, 5):
                got(oc.at[chunk], chunk, RX)
            got(near6, 6, RX)
            for k in (4, 5):
                got(zr.at[:, 0:HT, :], k, RZ)
            for i, result in enumerate((mlp, ing)):
                total = oc[NCH - 1, i] + xr[0, 2, i] + zr[i].astype(f32)
                result[0:HT, :] = (total[0:HT] + xr[0, 0, i, 0:HT] + xr[0, 1, i, 0:HT]).astype(bf16)
                result[HT:TOK, :] = (total[HT:TOK] + xr6[0, i].astype(f32) + xr6[1, i].astype(f32)).astype(bf16)

    def s12(c):
        @pl.when(c != NCH - 1)
        def _():
            sent(xall.at[c, :, :, 0:DL], c, AGX)

        @pl.when((c != NCH - 1) & (c != OTHER) & (c != 6))
        def _():
            sent(oc.at[c], c, RX)

        @pl.when(c == 6)
        def _():
            sent(near6, 6, RX)

        @pl.when((c == 4) | (c == 5))
        def _():
            sent(zr.at[:, 0:HT, :], c, RZ)

        sent(xall.at[c, :, :, 0:DL], c, AGC)
        for buf, kind in (
            (a_rel, A_REL), (a_dir, A_DIR), (a_sum, A_SUM), (a_z, A_Z),
            (b_z, B_Z), (b_rel, B_REL), (b_dir, B_DIR), (b_sum, B_SUM),
        ):
            sent(buf.at[c], c, kind)
        for rows, cols, kind in (
            (B, slice(0, WA), GA_Z), (4 * B, slice(0, WA), GA_1), (2 * B, slice(0, WA), GA_2),
            (2 * B, slice(WA, FH), GB_1), (B, slice(WA, FH), GB_2), (4 * B, slice(WA, FH), GB_Z),
        ):
            sent(hid.at[core, c, :, 0:rows, cols], c, kind)
        sent(hid.at[core, c, :, :, 0:WA], c, GC_A)
        sent(hid.at[core, c, :, :, WA:FH], c, GC_B)

    for copy in takes:
        copy.wait()
    gather()
    for copy in locals_:
        copy.start()
    for copy in swaps:
        copy.start()

    order = (
        (1, s3), (8, s10), (7, s9b), (7, s9a), (6, s8b), (4, s6a), (6, s8a), (0, s2),
        (5, s7b), (5, s7a), (3, s5b), (4, s6b), (2, s4b), (9, s11), (2, s4a), (3, s5a),
        (10, s12),
    )

    @pl.loop(0, NCH + STAGES - 1)
    def _(t):
        @pl.when((t >= FIRST) & (t < LAST))
        def _():
            early(t)

        for stage, work in order:

            @pl.when((t >= stage) & (t < stage + NCH))
            def _(stage=stage, work=work):
                work(t - stage)

    for copy in swaps:
        copy.wait_send()


TILE = 768


def gradients(mlp0, ing0, xt, down, hidt, grads, p_in, p_out, mlp, ing, wig, wog, g_in, g_out, sem):
    copies = [
        pltpu.make_async_copy(mlp0, mlp, sem.at[0, 0]),
        pltpu.make_async_copy(ing0, ing, sem.at[1, 0]),
    ]
    for copy in copies:
        copy.start()
    for j in range(FL // TILE):
        units = pl.ds(j * TILE, TILE)
        g_out[units, :] = p_out[units, :] + jnp.dot(hidt[units, :], down[...], preferred_element_type=f32)
        g_in[:, units] = p_in[:, units] + jnp.dot(xt[...], grads[:, units], preferred_element_type=f32)
        for copy in (
            pltpu.make_async_copy(g_out.at[units, :], wog.at[units, :], sem.at[0, j + 1]),
            pltpu.make_async_copy(g_in.at[:, units], wig.at[:, units], sem.at[1, j + 1]),
        ):
            copy.start()
            copies.append(copy)
    for copy in copies:
        copy.wait()


def on_device(tokens, w_in, w_out, out_grad):
    vmem, anywhere = pl.BlockSpec(memory_space=pltpu.VMEM), pl.BlockSpec(memory_space=pl.ANY)
    scratch = [
        ((NCH, 2, C, DC), bf16),
        ((DC, FH), bf16),
        ((FH, DC), bf16),
        ((DL, FL), bf16),
        ((FL, DL), bf16),
        ((NCH, 2, C, FH), bf16),
        ((NCH, 2, 2 * B, WA), bf16),
        ((NCH, 2, 2 * B, WA), bf16),
        ((NCH, 2, 2 * B, WA), bf16),
        ((NCH, 2, B, WA), bf16),
        ((NCH, 2, B, WA), bf16),
        ((NCH, 2, 4 * B, WB), bf16),
        ((NCH, 2, B, WB), bf16),
        ((NCH, 2, B, WB), bf16),
        ((NCH, 2, B, WB), bf16),
        ((2, NCH, 2, C, FH), bf16),
        ((NCH, 2, C, DL), f32),
        ((2, 3, 2, TOK, DL), f32),
        ((2, C, DL), bf16),
        ((2, 2, HT, DL), bf16),
        ((2, TOK, DL), bf16),
        ((2, TOK, DL), bf16),
    ]
    handed = [
        ((TOK, DL), bf16),
        ((TOK, DL), bf16),
        ((DL, HALF), bf16),
        ((HALF, DL), bf16),
        ((FL, HALF), bf16),
        ((HALF, FL), bf16),
        ((DL, FL), f32),
        ((FL, DL), f32),
    ]
    between = pl.pallas_call(
        kernel,
        out_shape=tuple(pltpu.VMEM(shape, dtype) for shape, dtype in handed),
        in_specs=[anywhere] * 4,
        out_specs=(vmem,) * len(handed),
        scratch_shapes=[pltpu.VMEM(shape, dtype) for shape, dtype in scratch]
        + [
            pltpu.SemaphoreType.DMA((NCH, KINDS)),
            pltpu.SemaphoreType.DMA((NCH, KINDS)),
            pltpu.SemaphoreType.DMA((4,)),
            pltpu.SemaphoreType.DMA((6,)),
        ],
        compiler_params=pltpu.CompilerParams(
            collective_id=0, has_side_effects=True, vmem_limit_bytes=45 * 2**20
        ),
    )(tokens, out_grad, w_in, w_out)
    between = [pltpu.with_memory_space_constraint(v, pltpu.VMEM) for v in between]
    return pl.pallas_call(
        gradients,
        out_shape=(
            jax.ShapeDtypeStruct((TOK, DL), bf16),
            jax.ShapeDtypeStruct((TOK, DL), bf16),
            jax.ShapeDtypeStruct((DL, FL), f32),
            jax.ShapeDtypeStruct((FL, DL), f32),
        ),
        in_specs=[vmem] * len(handed),
        out_specs=(anywhere,) * 4,
        scratch_shapes=[
            pltpu.VMEM((DL, FL), f32),
            pltpu.VMEM((FL, DL), f32),
            pltpu.SemaphoreType.DMA((2, FL // TILE + 1)),
        ],
        compiler_params=pltpu.CompilerParams(vmem_limit_bytes=12 * 2**20),
    )(*between)


def solution(mesh):
    in_specs = (P("row", "col"), P("col", "row"), P("row", "col"), P("row", "col"))
    out_specs = (P("row", "col"), P("row", "col"), P("col", "row"), P("row", "col"))
    return jax.shard_map(
        on_device, mesh=mesh, in_specs=in_specs, out_specs=out_specs, check_vma=False
    )
```

```python
import jax
import jax.numpy as jnp
from jax import lax
from jax.experimental import pallas as pl
from jax.experimental.pallas import tpu as pltpu
from jax.sharding import PartitionSpec as P

MESH = pl.DeviceIdType.MESH
f32, bf16 = jnp.float32, jnp.bfloat16
sqrt_half = 0.7071067811865476
inv_root = 0.3989422804014327

ROWS = 8
TOK = 128
DL = 384
DC = 768
FL = 3072
FH = 1536
NCH = 8
B = TOK // NCH
C = B * ROWS
WA, WB = 1024, 512
HA, HB = -(-WA // 256) * 128, -(-WB // 256) * 128
HT = TOK // 2
NEAR = {0: 0, 2: 0, 4: HT, 6: HT}
FAR = (5, 3)
OTHER = 1
STAGES = 11
FIRST, LAST = 11, 15
HALF = NCH // 2 * C

(AGX, AGC, A_REL, A_DIR, A_SUM, A_Z, B_Z, B_REL, B_DIR, B_SUM, GA_Z, GA_1, GA_2, GB_1, GB_2, GB_Z, GC_A, GC_B, RX, RZ) = range(20)
KINDS = 20


def kernel(
    tok, dy, w_in, w_out,
    mlp, ing, xt, down, hidt, grads, p_in, p_out,
    xall, wih, woh, winv, woutv, part,
    a_rel, a_dir, a_sum, a_out, a_z, b_z, b_rel, b_dir, b_sum,
    hid, oc, xr, near6, xr6, zs, zr,
    ssem, rsem, wsem, lsem,
):
    row, col = lax.axis_index("row"), lax.axis_index("col")
    x, zh = row // 2, row % 2
    zl, y, core = col // 8, (col // 2) % 4, col % 2
    other = 1 - core

    def dev(dx=0, dzh=0, dzl=0, dyy=0, dc=0):
        return (
            ((x + dx) % 4) * 2 + (zh + dzh) % 2,
            (((zl + dzl) % 2) * 4 + (y + dyy) % 4) * 2 + (core + dc) % 2,
        )

    XP, XM, XO = dev(dx=1), dev(dx=3), dev(dx=2)
    ZH, ZL = dev(dzh=1), dev(dzl=1)
    YP, YM = dev(dyy=1), dev(dyy=3)
    CO = dev(dc=1)
    yr, yl, yo = (y + 1) % 4, (y + 3) % 4, (y + 2) % 4

    def send(src, dst, c, kind, to):
        pltpu.make_async_remote_copy(
            src_ref=src, dst_ref=dst, send_sem=ssem.at[c, kind], recv_sem=rsem.at[c, kind],
            device_id=to, device_id_type=MESH,
        ).start()

    def got(view, c, kind):
        pltpu.make_async_copy(view, view, rsem.at[c, kind]).wait()

    def sent(view, c, kind):
        pltpu.make_async_copy(view, view, ssem.at[c, kind]).wait()

    def ds(i, size):
        return pl.ds(pl.multiple_of(i * size, size), size)

    barrier = pltpu.get_barrier_semaphore()
    for d in (XP, XM, XO, ZH, ZL, YP, YM, CO):
        pl.semaphore_signal(barrier, 1, device_id=d, device_id_type=MESH)
    takes = [
        pltpu.make_async_copy(src, xall.at[NCH - 1, i, :, 0:DL], lsem.at[4 + i]) for i, src in enumerate((tok, dy))
    ]
    for copy in takes:
        copy.start()
    pl.semaphore_wait(barrier, 8)

    swaps = [
        pltpu.make_async_remote_copy(
            src_ref=w_in.at[:, ds(other, FH)], dst_ref=wih.at[pl.ds(DL, DL), :],
            send_sem=wsem.at[0], recv_sem=wsem.at[1], device_id=CO, device_id_type=MESH,
        ),
        pltpu.make_async_remote_copy(
            src_ref=w_out.at[ds(other, FH), :], dst_ref=woh.at[:, pl.ds(DL, DL)],
            send_sem=wsem.at[2], recv_sem=wsem.at[3], device_id=CO, device_id_type=MESH,
        ),
    ]
    locals_ = [
        pltpu.make_async_copy(w_in.at[:, ds(core, FH)], wih.at[pl.ds(0, DL), :], lsem.at[0]),
        pltpu.make_async_copy(w_out.at[ds(core, FH), :], woh.at[:, pl.ds(0, DL)], lsem.at[1]),
        pltpu.make_async_copy(w_in, winv, lsem.at[2]),
        pltpu.make_async_copy(w_out, woutv, lsem.at[3]),
    ]
    def near(c, src):
        half = pl.ds(NEAR[c], HT)
        send(xall.at[src, :, half, 0:DL], xall.at[c, :, pl.ds(0, HT), 0:DL], c, AGX, XM)
        send(xall.at[src, :, half, 0:DL], xall.at[c, :, pl.ds(HT, HT), 0:DL], c, AGX, XP)

    def whole(c, src, to):
        send(xall.at[src, :, :, 0:DL], xall.at[c, :, :, 0:DL], c, AGX, to)

    def gather():
        near(0, NCH - 1)
        whole(OTHER, NCH - 1, ZH)

    def forward():
        got(xall.at[OTHER, :, :, 0:DL], OTHER, AGX)
        near(2, OTHER)
        whole(FAR[1], OTHER, XO)
        near(4, OTHER)
        whole(FAR[0], NCH - 1, XO)
        near(6, NCH - 1)

    def s2(c):
        pl.when(c == OTHER)(forward)

        @pl.when((c != OTHER) & (c != NCH - 1))
        def _():
            got(xall.at[c, :, :, 0:DL], c, AGX)

        send(xall.at[c, :, :, 0:DL], xall.at[c, :, :, DL:DC], c, AGC, CO)

    def y_rows(d, rows, off):
        return pl.ds(pl.multiple_of(d * rows + off, B), rows)

    def y_send(c, rows, off, c0, cut, c1, rel, direct, krel, kdir):
        h = cut - c0
        for i, (half, place) in enumerate(((pl.ds(c0, h), pl.ds(0, h)), (pl.ds(cut, c1 - cut), pl.ds(h, c1 - cut)))):
            send(part.at[c, :, y_rows(yo, rows, off), half], rel.at[c, :, :, place], c, krel, (YP, YM)[i])
            d, to = ((yl, YM), (yr, YP))[i]
            send(part.at[c, :, y_rows(d, rows, off), half], direct.at[c, :, :, place], c, kdir, to)

    def y_relay(c, rows, off, c0, cut, c1, rel, total, krel, ksum):
        got(rel.at[c], c, krel)
        h = cut - c0
        for half, at, d, to in (
            (pl.ds(c0, h), pl.ds(0, h), yr, YP), (pl.ds(cut, c1 - cut), pl.ds(h, c1 - cut), yl, YM),
        ):
            place = (c, slice(None), y_rows(d, rows, off), half)
            part[place] = (part[place].astype(f32) + rel[c, :, :, at].astype(f32)).astype(bf16)
            send(part.at[place], total.at[c, :, :, at], c, ksum, to)

    def y_total(c, rows, off, sub, c0, c1, direct, total):
        own = part[c, :, pl.ds(pl.multiple_of(y * rows + off + sub, B), B), c0:c1]
        at = pl.ds(pl.multiple_of(sub, B), B)
        return own.astype(f32) + direct[c, :, at, :].astype(f32) + total[c, :, at, :].astype(f32)

    off_b = zl * (4 * B)
    route_a = (2 * B, 0, 0, HA, WA)
    route_b = (B, off_b, WA, WA + HB, FH)
    a_mine, b_mine = ds(y * 2 + zl, B), ds(zl * 4 + y, B)

    def s3(c):
        @pl.when(c == 0)
        def _():
            for copy in locals_[:2]:
                copy.wait()
            for copy in swaps:
                copy.wait_recv()

        got(xall.at[c, :, :, DL:DC], c, AGC)

        def products(first, end):
            @pl.loop(first, end)
            def _(j):
                cols = ds(j, 256)
                part[c, 0, :, cols] = jnp.dot(
                    xall[c, 0], wih[:, cols], preferred_element_type=f32
                ).astype(bf16)
                part[c, 1, :, cols] = lax.dot_general(
                    xall[c, 1], woh[cols, :], (((1,), (1,)), ((), ())), preferred_element_type=f32
                ).astype(bf16)

        products(0, -(-WA // 256))
        y_send(c, *route_a, a_rel, a_dir, A_REL, A_DIR)
        products(-(-WA // 256), FH // 256)
        send(part.at[c, :, ds(1 - zl, 4 * B), WA:FH], b_z.at[c], c, B_Z, ZL)

    def s4a(c):
        y_relay(c, *route_a, a_rel, a_sum, A_REL, A_SUM)

    def s4b(c):
        got(b_z.at[c], c, B_Z)
        place = (c, slice(None), ds(zl, 4 * B), slice(WA, FH))
        part[place] = (part[place].astype(f32) + b_z[c].astype(f32)).astype(bf16)
        y_send(c, *route_b, b_rel, b_dir, B_REL, B_DIR)

    def s5a(c):
        got(a_dir.at[c], c, A_DIR)
        got(a_sum.at[c], c, A_SUM)
        a_out[c] = y_total(c, 2 * B, 0, (1 - zl) * B, 0, WA, a_dir, a_sum).astype(bf16)
        send(a_out.at[c], a_z.at[c], c, A_Z, ZL)

    def s5b(c):
        y_relay(c, *route_b, b_rel, b_sum, B_REL, B_SUM)

    def unit(c, rows, c0, c1, both):
        pre, grad = both[0], both[1]
        half_erf = 0.5 * (1.0 + lax.erf(pre * sqrt_half))
        hid[core, c, 0, rows, c0:c1] = (pre * half_erf).astype(bf16)
        slope = half_erf + pre * jnp.exp(-0.5 * pre * pre) * inv_root
        hid[core, c, 1, rows, c0:c1] = (grad * slope).astype(bf16)

    def s6a(c):
        got(a_z.at[c], c, A_Z)
        unit(c, a_mine, 0, WA, y_total(c, 2 * B, 0, zl * B, 0, WA, a_dir, a_sum) + a_z[c].astype(f32))
        view = hid.at[core, c, :, a_mine, 0:WA]
        send(view, view, c, GA_Z, ZL)

    def s6b(c):
        got(b_dir.at[c], c, B_DIR)
        got(b_sum.at[c], c, B_SUM)
        unit(c, b_mine, WA, FH, y_total(c, B, off_b, 0, WA, FH, b_dir, b_sum))
        view = hid.at[core, c, :, b_mine, WA:FH]
        send(view, view, c, GB_1, YP)
        send(view, view, c, GB_1, YM)

    def y_forward(c, rows, off, c0, cut, c1, kind):
        for d, half, to in ((yl, pl.ds(c0, cut - c0), YP), (yr, pl.ds(cut, c1 - cut), YM)):
            view = hid.at[core, c, :, y_rows(d, rows, off), half]
            send(view, view, c, kind, to)

    def s7a(c):
        got(hid.at[core, c, :, ds(y * 2 + 1 - zl, B), 0:WA], c, GA_Z)
        view = hid.at[core, c, :, ds(y, 2 * B), 0:WA]
        send(view, view, c, GA_1, YP)
        send(view, view, c, GA_1, YM)

    def s7b(c):
        got(hid.at[core, c, :, 0 : 2 * B, WA:FH], c, GB_1)
        y_forward(c, *route_b, GB_2)

    def s8a(c):
        got(hid.at[core, c, :, 0 : 4 * B, 0:WA], c, GA_1)
        y_forward(c, *route_a, GA_2)

    def s8b(c):
        got(hid.at[core, c, :, 0:B, WA:FH], c, GB_2)
        view = hid.at[core, c, :, ds(zl, 4 * B), WA:FH]
        send(view, view, c, GB_Z, ZL)

    def s9a(c):
        got(hid.at[core, c, :, 0 : 2 * B, 0:WA], c, GA_2)
        send(hid.at[core, c, :, :, 0:WA], hid.at[core, c, :, :, 0:WA], c, GC_A, CO)

    def s9b(c):
        got(hid.at[core, c, :, 0 : 4 * B, WA:FH], c, GB_Z)
        send(hid.at[core, c, :, :, WA:FH], hid.at[core, c, :, :, WA:FH], c, GC_B, CO)

    def s10(c):
        @pl.when(c == 0)
        def _():
            for copy in locals_[2:]:
                copy.wait()

        def products(half):
            units = ds(half, FH)
            out = jnp.dot(hid[half, c, 0], woutv[units, :], preferred_element_type=f32)
            back = lax.dot_general(
                hid[half, c, 1], winv[:, units], (((1,), (1,)), ((), ())), preferred_element_type=f32
            )
            return out, back

        oc[c, 0], oc[c, 1] = products(core)
        got(hid.at[other, c, :, :, 0:WA], c, GC_A)
        got(hid.at[other, c, :, :, WA:FH], c, GC_B)
        out, back = products(other)
        oc[c, 0] += out
        oc[c, 1] += back
        for k, first in NEAR.items():
            if k == 6:
                continue

            @pl.when(c == k)
            def _(k=k, first=first):
                for i, to in enumerate((XP, XM)):
                    dst = xr.at[int(k in (2, 4)), i, :, pl.ds(first, HT), :]
                    send(oc.at[k, :, pl.ds(i * HT, HT), :], dst, k, RX, to)

        @pl.when(c == 6)
        def _():
            near6[...] = oc[6].astype(bf16)
            for i, to in enumerate((XP, XM)):
                send(near6.at[:, pl.ds(i * HT, HT), :], xr6.at[i], 6, RX, to)

        for k in FAR:

            @pl.when(c == k)
            def _(k=k):
                send(oc.at[k], xr.at[FAR.index(k), 2], k, RX, XO)

        @pl.when(c >= NCH // 2)
        def _():
            tokens = ds(c - NCH // 2, C)
            for k in range(2):
                hidt[k * FH : (k + 1) * FH, tokens] = hid[k, c, 0].T
                grads[tokens, k * FH : (k + 1) * FH] = hid[k, c, 1]
            xt[:, tokens] = xall[c, 0, :, 0:DL].T
            down[tokens, :] = xall[c, 1, :, 0:DL]

    def early(t):
        tiles = FL // 256 // (LAST - FIRST)
        first = pl.ds(0, NCH // 2)
        tn = (((0,), (0,)), ((), ()))
        up_t = xall[first, 0, :, 0:DL].reshape(HALF, DL).T

        @pl.loop(0, tiles)
        def _(i):
            j = (t - FIRST) * tiles + i
            units, k, place = ds(j, 256), j // 6, ds(j % 6, 256)
            p_out[units, :] = lax.dot_general(
                hid[k, first, 0, :, place].reshape(HALF, 256),
                xall[first, 1, :, 0:DL].reshape(HALF, DL),
                tn,
                preferred_element_type=f32,
            )
            p_in[:, units] = jnp.dot(
                up_t, hid[k, first, 1, :, place].reshape(HALF, 256), preferred_element_type=f32
            )

    def s11(c):
        for k, chunks, first in ((4, (2, 3), 0), (5, (4,), HT)):

            @pl.when(c == k)
            def _(k=k, chunks=chunks, first=first):
                for chunk in chunks:
                    got(oc.at[chunk], chunk, RX)
                half = pl.ds(first, HT)
                total = oc[OTHER, :, half, :] + xr[1, 2, :, half, :]
                zs[:, half, :] = (total + xr[1, 0, :, half, :] + xr[1, 1, :, half, :]).astype(bf16)
                send(zs.at[:, half, :], zr.at[:, half, :], k, RZ, ZH)

        @pl.when(c == NCH - 1)
        def _():
            for chunk in (0, 5):
                got(oc.at[chunk], chunk, RX)
            got(near6, 6, RX)
            for k in (4, 5):
                got(zr.at[:, 0:HT, :], k, RZ)
            for i, result in enumerate((mlp, ing)):
                total = oc[NCH - 1, i] + xr[0, 2, i] + zr[i].astype(f32)
                result[0:HT, :] = (total[0:HT] + xr[0, 0, i, 0:HT] + xr[0, 1, i, 0:HT]).astype(bf16)
                result[HT:TOK, :] = (total[HT:TOK] + xr6[0, i].astype(f32) + xr6[1, i].astype(f32)).astype(bf16)

    def s12(c):
        @pl.when(c != NCH - 1)
        def _():
            sent(xall.at[c, :, :, 0:DL], c, AGX)

        @pl.when((c != NCH - 1) & (c != OTHER) & (c != 6))
        def _():
            sent(oc.at[c], c, RX)

        @pl.when(c == 6)
        def _():
            sent(near6, 6, RX)

        @pl.when((c == 4) | (c == 5))
        def _():
            sent(zr.at[:, 0:HT, :], c, RZ)

        sent(xall.at[c, :, :, 0:DL], c, AGC)
        for buf, kind in (
            (a_rel, A_REL), (a_dir, A_DIR), (a_sum, A_SUM), (a_z, A_Z),
            (b_z, B_Z), (b_rel, B_REL), (b_dir, B_DIR), (b_sum, B_SUM),
        ):
            sent(buf.at[c], c, kind)
        for rows, cols, kind in (
            (B, slice(0, WA), GA_Z), (4 * B, slice(0, WA), GA_1), (2 * B, slice(0, WA), GA_2),
            (2 * B, slice(WA, FH), GB_1), (B, slice(WA, FH), GB_2), (4 * B, slice(WA, FH), GB_Z),
        ):
            sent(hid.at[core, c, :, 0:rows, cols], c, kind)
        sent(hid.at[core, c, :, :, 0:WA], c, GC_A)
        sent(hid.at[core, c, :, :, WA:FH], c, GC_B)

    for copy in takes:
        copy.wait()
    gather()
    for copy in swaps:
        copy.start()
    for copy in locals_:
        copy.start()

    order = (
        (9, s11), (7, s9a), (7, s9b), (6, s8a), (5, s7a), (6, s8b), (7, s10), (1, s3),
        (0, s2), (5, s7b), (4, s6a), (4, s6b), (2, s4b), (2, s4a), (3, s5a), (3, s5b),
        (10, s12),
    )

    @pl.loop(0, NCH + STAGES - 1)
    def _(t):
        @pl.when((t >= FIRST) & (t < LAST))
        def _():
            early(t)

        for stage, work in order:

            @pl.when((t >= stage) & (t < stage + NCH))
            def _(stage=stage, work=work):
                work(t - stage)

    for copy in swaps:
        copy.wait_send()


TILE = 512


def gradients(mlp0, ing0, xt, down, hidt, grads, p_in, p_out, mlp, ing, wig, wog, g_in, g_out, sem):
    copies = [
        pltpu.make_async_copy(mlp0, mlp, sem.at[0, 0]),
        pltpu.make_async_copy(ing0, ing, sem.at[1, 0]),
    ]
    for copy in copies:
        copy.start()
    for j in range(FL // TILE):
        units = pl.ds(j * TILE, TILE)
        g_out[units, :] = p_out[units, :] + jnp.dot(hidt[units, :], down[...], preferred_element_type=f32)
        g_in[:, units] = p_in[:, units] + jnp.dot(xt[...], grads[:, units], preferred_element_type=f32)
        for copy in (
            pltpu.make_async_copy(g_out.at[units, :], wog.at[units, :], sem.at[0, j + 1]),
            pltpu.make_async_copy(g_in.at[:, units], wig.at[:, units], sem.at[1, j + 1]),
        ):
            copy.start()
            copies.append(copy)
    for copy in copies:
        copy.wait()


def on_device(tokens, w_in, w_out, out_grad):
    vmem, anywhere = pl.BlockSpec(memory_space=pltpu.VMEM), pl.BlockSpec(memory_space=pl.ANY)
    scratch = [
        ((NCH, 2, C, DC), bf16),
        ((DC, FH), bf16),
        ((FH, DC), bf16),
        ((DL, FL), bf16),
        ((FL, DL), bf16),
        ((NCH, 2, C, FH), bf16),
        ((NCH, 2, 2 * B, WA), bf16),
        ((NCH, 2, 2 * B, WA), bf16),
        ((NCH, 2, 2 * B, WA), bf16),
        ((NCH, 2, B, WA), bf16),
        ((NCH, 2, B, WA), bf16),
        ((NCH, 2, 4 * B, WB), bf16),
        ((NCH, 2, B, WB), bf16),
        ((NCH, 2, B, WB), bf16),
        ((NCH, 2, B, WB), bf16),
        ((2, NCH, 2, C, FH), bf16),
        ((NCH, 2, C, DL), f32),
        ((2, 3, 2, TOK, DL), f32),
        ((2, C, DL), bf16),
        ((2, 2, HT, DL), bf16),
        ((2, TOK, DL), bf16),
        ((2, TOK, DL), bf16),
    ]
    handed = [
        ((TOK, DL), bf16),
        ((TOK, DL), bf16),
        ((DL, HALF), bf16),
        ((HALF, DL), bf16),
        ((FL, HALF), bf16),
        ((HALF, FL), bf16),
        ((DL, FL), f32),
        ((FL, DL), f32),
    ]
    between = pl.pallas_call(
        kernel,
        out_shape=tuple(pltpu.VMEM(shape, dtype) for shape, dtype in handed),
        in_specs=[anywhere] * 4,
        out_specs=(vmem,) * len(handed),
        scratch_shapes=[pltpu.VMEM(shape, dtype) for shape, dtype in scratch]
        + [
            pltpu.SemaphoreType.DMA((NCH, KINDS)),
            pltpu.SemaphoreType.DMA((NCH, KINDS)),
            pltpu.SemaphoreType.DMA((4,)),
            pltpu.SemaphoreType.DMA((6,)),
        ],
        compiler_params=pltpu.CompilerParams(
            collective_id=0, has_side_effects=True, vmem_limit_bytes=45 * 2**20
        ),
    )(tokens, out_grad, w_in, w_out)
    between = [pltpu.with_memory_space_constraint(v, pltpu.VMEM) for v in between]
    return pl.pallas_call(
        gradients,
        out_shape=(
            jax.ShapeDtypeStruct((TOK, DL), bf16),
            jax.ShapeDtypeStruct((TOK, DL), bf16),
            jax.ShapeDtypeStruct((DL, FL), f32),
            jax.ShapeDtypeStruct((FL, DL), f32),
        ),
        in_specs=[vmem] * len(handed),
        out_specs=(anywhere,) * 4,
        scratch_shapes=[
            pltpu.VMEM((DL, FL), f32),
            pltpu.VMEM((FL, DL), f32),
            pltpu.SemaphoreType.DMA((2, FL // TILE + 1)),
        ],
        compiler_params=pltpu.CompilerParams(vmem_limit_bytes=12 * 2**20),
    )(*between)


def solution(mesh):
    in_specs = (P("row", "col"), P("col", "row"), P("row", "col"), P("row", "col"))
    out_specs = (P("row", "col"), P("row", "col"), P("col", "row"), P("row", "col"))
    return jax.shard_map(
        on_device, mesh=mesh, in_specs=in_specs, out_specs=out_specs, check_vma=False
    )
```

```python
import jax
import jax.numpy as jnp
from jax import lax
from jax.experimental import pallas as pl
from jax.experimental.pallas import tpu as pltpu
from jax.sharding import PartitionSpec as P

MESH = pl.DeviceIdType.MESH
f32, bf16 = jnp.float32, jnp.bfloat16
sqrt_half = 0.7071067811865476
inv_root = 0.3989422804014327

ROWS = 8
TOK = 128
DL = 384
DC = 768
FL = 3072
FH = 1536
NCH = 8
B = TOK // NCH
C = B * ROWS
WA, WB = 1024, 512
HA, HB = -(-WA // 256) * 128, -(-WB // 256) * 128
HT = TOK // 2
NEAR = {0: 0, 2: 0, 4: HT, 6: HT}
FAR = (5, 3)
OTHER = 1
STAGES = 10
FIRST, LAST = 11, 15
HALF = NCH // 2 * C

(AGX, AGC, A_REL, A_DIR, A_SUM, A_Z, B_Z, B_REL, B_DIR, B_SUM, GA_Z, GA_1, GA_2, GB_1, GB_2, GB_Z, GC_A, GC_B, RX, RZ) = range(20)
KINDS = 20


def kernel(
    tok, dy, w_in, w_out,
    mlp, ing, xt, down, hidt, grads, p_in, p_out,
    xall, wih, woh, winv, woutv, part,
    a_rel, a_dir, a_sum, a_out, a_z, b_z, b_rel, b_dir, b_sum,
    hid, oc, xr, near6, xr6, zs, zr,
    ssem, rsem, wsem, lsem,
):
    row, col = lax.axis_index("row"), lax.axis_index("col")
    x, zh = row // 2, row % 2
    zl, y, core = col // 8, (col // 2) % 4, col % 2
    other = 1 - core

    def dev(dx=0, dzh=0, dzl=0, dyy=0, dc=0):
        return (
            ((x + dx) % 4) * 2 + (zh + dzh) % 2,
            (((zl + dzl) % 2) * 4 + (y + dyy) % 4) * 2 + (core + dc) % 2,
        )

    XP, XM, XO = dev(dx=1), dev(dx=3), dev(dx=2)
    ZH, ZL = dev(dzh=1), dev(dzl=1)
    YP, YM = dev(dyy=1), dev(dyy=3)
    CO = dev(dc=1)
    yr, yl, yo = (y + 1) % 4, (y + 3) % 4, (y + 2) % 4

    def send(src, dst, c, kind, to):
        pltpu.make_async_remote_copy(
            src_ref=src, dst_ref=dst, send_sem=ssem.at[c, kind], recv_sem=rsem.at[c, kind],
            device_id=to, device_id_type=MESH,
        ).start()

    def got(view, c, kind):
        pltpu.make_async_copy(view, view, rsem.at[c, kind]).wait()

    def sent(view, c, kind):
        pltpu.make_async_copy(view, view, ssem.at[c, kind]).wait()

    def ds(i, size):
        return pl.ds(pl.multiple_of(i * size, size), size)

    barrier = pltpu.get_barrier_semaphore()
    for d in (XP, XM, XO, ZH, ZL, YP, YM, CO):
        pl.semaphore_signal(barrier, 1, device_id=d, device_id_type=MESH)
    takes = [
        pltpu.make_async_copy(src, xall.at[NCH - 1, i, :, 0:DL], lsem.at[4 + i]) for i, src in enumerate((tok, dy))
    ]
    for copy in takes:
        copy.start()
    pl.semaphore_wait(barrier, 8)

    swaps = [
        pltpu.make_async_remote_copy(
            src_ref=w_in.at[:, ds(other, FH)], dst_ref=wih.at[pl.ds(DL, DL), :],
            send_sem=wsem.at[0], recv_sem=wsem.at[1], device_id=CO, device_id_type=MESH,
        ),
        pltpu.make_async_remote_copy(
            src_ref=w_out.at[ds(other, FH), :], dst_ref=woh.at[:, pl.ds(DL, DL)],
            send_sem=wsem.at[2], recv_sem=wsem.at[3], device_id=CO, device_id_type=MESH,
        ),
    ]
    locals_ = [
        pltpu.make_async_copy(w_in.at[:, ds(core, FH)], wih.at[pl.ds(0, DL), :], lsem.at[0]),
        pltpu.make_async_copy(w_out.at[ds(core, FH), :], woh.at[:, pl.ds(0, DL)], lsem.at[1]),
        pltpu.make_async_copy(w_in, winv, lsem.at[2]),
        pltpu.make_async_copy(w_out, woutv, lsem.at[3]),
    ]
    def near(c, src):
        half = pl.ds(NEAR[c], HT)
        send(xall.at[src, :, half, 0:DL], xall.at[c, :, pl.ds(0, HT), 0:DL], c, AGX, XM)
        send(xall.at[src, :, half, 0:DL], xall.at[c, :, pl.ds(HT, HT), 0:DL], c, AGX, XP)

    def whole(c, src, to):
        send(xall.at[src, :, :, 0:DL], xall.at[c, :, :, 0:DL], c, AGX, to)

    def gather():
        near(0, NCH - 1)
        whole(OTHER, NCH - 1, ZH)

    def forward():
        got(xall.at[OTHER, :, :, 0:DL], OTHER, AGX)
        near(2, OTHER)
        whole(FAR[1], OTHER, XO)
        near(4, OTHER)
        whole(FAR[0], NCH - 1, XO)
        near(6, NCH - 1)

    def s2(c):
        pl.when(c == OTHER)(forward)

        @pl.when((c != OTHER) & (c != NCH - 1))
        def _():
            got(xall.at[c, :, :, 0:DL], c, AGX)

        send(xall.at[c, :, :, 0:DL], xall.at[c, :, :, DL:DC], c, AGC, CO)

    def y_rows(d, rows, off):
        return pl.ds(pl.multiple_of(d * rows + off, B), rows)

    def y_send(c, rows, off, c0, cut, c1, rel, direct, krel, kdir):
        h = cut - c0
        for i, (half, place) in enumerate(((pl.ds(c0, h), pl.ds(0, h)), (pl.ds(cut, c1 - cut), pl.ds(h, c1 - cut)))):
            send(part.at[c, :, y_rows(yo, rows, off), half], rel.at[c, :, :, place], c, krel, (YP, YM)[i])
            d, to = ((yl, YM), (yr, YP))[i]
            send(part.at[c, :, y_rows(d, rows, off), half], direct.at[c, :, :, place], c, kdir, to)

    def y_relay(c, rows, off, c0, cut, c1, rel, total, krel, ksum):
        got(rel.at[c], c, krel)
        h = cut - c0
        for half, at, d, to in (
            (pl.ds(c0, h), pl.ds(0, h), yr, YP), (pl.ds(cut, c1 - cut), pl.ds(h, c1 - cut), yl, YM),
        ):
            place = (c, slice(None), y_rows(d, rows, off), half)
            part[place] = (part[place].astype(f32) + rel[c, :, :, at].astype(f32)).astype(bf16)
            send(part.at[place], total.at[c, :, :, at], c, ksum, to)

    def y_total(c, rows, off, sub, c0, c1, direct, total):
        own = part[c, :, pl.ds(pl.multiple_of(y * rows + off + sub, B), B), c0:c1]
        at = pl.ds(pl.multiple_of(sub, B), B)
        return own.astype(f32) + direct[c, :, at, :].astype(f32) + total[c, :, at, :].astype(f32)

    off_b = zl * (4 * B)
    route_a = (2 * B, 0, 0, HA, WA)
    route_b = (B, off_b, WA, WA + HB, FH)
    a_mine, b_mine = ds(y * 2 + zl, B), ds(zl * 4 + y, B)

    def s3(c):
        @pl.when(c == 0)
        def _():
            for copy in locals_[:2]:
                copy.wait()
            for copy in swaps:
                copy.wait_recv()

        got(xall.at[c, :, :, DL:DC], c, AGC)

        def products(first, end):
            @pl.loop(first, end)
            def _(j):
                cols = ds(j, 256)
                part[c, 0, :, cols] = jnp.dot(
                    xall[c, 0], wih[:, cols], preferred_element_type=f32
                ).astype(bf16)
                part[c, 1, :, cols] = lax.dot_general(
                    xall[c, 1], woh[cols, :], (((1,), (1,)), ((), ())), preferred_element_type=f32
                ).astype(bf16)

        products(0, -(-WA // 256))
        y_send(c, *route_a, a_rel, a_dir, A_REL, A_DIR)
        products(-(-WA // 256), FH // 256)
        send(part.at[c, :, ds(1 - zl, 4 * B), WA:FH], b_z.at[c], c, B_Z, ZL)

    def s4a(c):
        y_relay(c, *route_a, a_rel, a_sum, A_REL, A_SUM)

    def s4b(c):
        got(b_z.at[c], c, B_Z)
        place = (c, slice(None), ds(zl, 4 * B), slice(WA, FH))
        part[place] = (part[place].astype(f32) + b_z[c].astype(f32)).astype(bf16)
        y_send(c, *route_b, b_rel, b_dir, B_REL, B_DIR)

    def s5a(c):
        got(a_dir.at[c], c, A_DIR)
        got(a_sum.at[c], c, A_SUM)
        a_out[c] = y_total(c, 2 * B, 0, (1 - zl) * B, 0, WA, a_dir, a_sum).astype(bf16)
        send(a_out.at[c], a_z.at[c], c, A_Z, ZL)

    def s5b(c):
        y_relay(c, *route_b, b_rel, b_sum, B_REL, B_SUM)

    def unit(c, rows, c0, c1, both):
        pre, grad = both[0], both[1]
        half_erf = 0.5 * (1.0 + lax.erf(pre * sqrt_half))
        hid[core, c, 0, rows, c0:c1] = (pre * half_erf).astype(bf16)
        slope = half_erf + pre * jnp.exp(-0.5 * pre * pre) * inv_root
        hid[core, c, 1, rows, c0:c1] = (grad * slope).astype(bf16)

    def s6a(c):
        got(a_z.at[c], c, A_Z)
        unit(c, a_mine, 0, WA, y_total(c, 2 * B, 0, zl * B, 0, WA, a_dir, a_sum) + a_z[c].astype(f32))
        view = hid.at[core, c, :, a_mine, 0:WA]
        send(view, view, c, GA_Z, ZL)

    def s6b(c):
        got(b_dir.at[c], c, B_DIR)
        got(b_sum.at[c], c, B_SUM)
        unit(c, b_mine, WA, FH, y_total(c, B, off_b, 0, WA, FH, b_dir, b_sum))
        view = hid.at[core, c, :, b_mine, WA:FH]
        send(view, view, c, GB_1, YP)
        send(view, view, c, GB_1, YM)

    def y_forward(c, rows, off, c0, cut, c1, kind):
        for d, half, to in ((yl, pl.ds(c0, cut - c0), YP), (yr, pl.ds(cut, c1 - cut), YM)):
            view = hid.at[core, c, :, y_rows(d, rows, off), half]
            send(view, view, c, kind, to)

    def s7a(c):
        got(hid.at[core, c, :, ds(y * 2 + 1 - zl, B), 0:WA], c, GA_Z)
        view = hid.at[core, c, :, ds(y, 2 * B), 0:WA]
        send(view, view, c, GA_1, YP)
        send(view, view, c, GA_1, YM)

    def s7b(c):
        got(hid.at[core, c, :, 0 : 2 * B, WA:FH], c, GB_1)
        y_forward(c, *route_b, GB_2)

    def s8a(c):
        got(hid.at[core, c, :, 0 : 4 * B, 0:WA], c, GA_1)
        y_forward(c, *route_a, GA_2)

    def s8b(c):
        got(hid.at[core, c, :, 0:B, WA:FH], c, GB_2)
        view = hid.at[core, c, :, ds(zl, 4 * B), WA:FH]
        send(view, view, c, GB_Z, ZL)

    def s9a(c):
        got(hid.at[core, c, :, 0 : 2 * B, 0:WA], c, GA_2)
        send(hid.at[core, c, :, :, 0:WA], hid.at[core, c, :, :, 0:WA], c, GC_A, CO)

    def s9b(c):
        got(hid.at[core, c, :, 0 : 4 * B, WA:FH], c, GB_Z)
        send(hid.at[core, c, :, :, WA:FH], hid.at[core, c, :, :, WA:FH], c, GC_B, CO)

    def s10(c):
        @pl.when(c == 0)
        def _():
            for copy in locals_[2:]:
                copy.wait()

        def products(half):
            units = ds(half, FH)
            out = jnp.dot(hid[half, c, 0], woutv[units, :], preferred_element_type=f32)
            back = lax.dot_general(
                hid[half, c, 1], winv[:, units], (((1,), (1,)), ((), ())), preferred_element_type=f32
            )
            return out, back

        oc[c, 0], oc[c, 1] = products(core)
        got(hid.at[other, c, :, :, 0:WA], c, GC_A)
        got(hid.at[other, c, :, :, WA:FH], c, GC_B)
        out, back = products(other)
        oc[c, 0] += out
        oc[c, 1] += back
        for k, first in NEAR.items():
            if k == 6:
                continue

            @pl.when(c == k)
            def _(k=k, first=first):
                for i, to in enumerate((XP, XM)):
                    dst = xr.at[int(k in (2, 4)), i, :, pl.ds(first, HT), :]
                    send(oc.at[k, :, pl.ds(i * HT, HT), :], dst, k, RX, to)

        @pl.when(c == 6)
        def _():
            near6[...] = oc[6].astype(bf16)
            for i, to in enumerate((XP, XM)):
                send(near6.at[:, pl.ds(i * HT, HT), :], xr6.at[i], 6, RX, to)

        for k in FAR:

            @pl.when(c == k)
            def _(k=k):
                send(oc.at[k], xr.at[FAR.index(k), 2], k, RX, XO)

        @pl.when(c >= NCH // 2)
        def _():
            tokens = ds(c - NCH // 2, C)
            for k in range(2):
                hidt[k * FH : (k + 1) * FH, tokens] = hid[k, c, 0].T
                grads[tokens, k * FH : (k + 1) * FH] = hid[k, c, 1]
            xt[:, tokens] = xall[c, 0, :, 0:DL].T
            down[tokens, :] = xall[c, 1, :, 0:DL]

    def early(t):
        tiles = FL // 256 // (LAST - FIRST)
        first = pl.ds(0, NCH // 2)
        tn = (((0,), (0,)), ((), ()))
        up_t = xall[first, 0, :, 0:DL].reshape(HALF, DL).T

        @pl.loop(0, tiles)
        def _(i):
            j = (t - FIRST) * tiles + i
            units, k, place = ds(j, 256), j // 6, ds(j % 6, 256)
            p_out[units, :] = lax.dot_general(
                hid[k, first, 0, :, place].reshape(HALF, 256),
                xall[first, 1, :, 0:DL].reshape(HALF, DL),
                tn,
                preferred_element_type=f32,
            )
            p_in[:, units] = jnp.dot(
                up_t, hid[k, first, 1, :, place].reshape(HALF, 256), preferred_element_type=f32
            )

    def settle(c):
        @pl.when(c != NCH - 1)
        def _():
            sent(xall.at[c, :, :, 0:DL], c, AGX)

        @pl.when((c != NCH - 1) & (c != OTHER) & (c != 6))
        def _():
            sent(oc.at[c], c, RX)

        @pl.when(c == 6)
        def _():
            sent(near6, 6, RX)

        @pl.when((c == 5) | (c == 6))
        def _():
            sent(zr.at[:, 0:HT, :], c - 1, RZ)

        sent(xall.at[c, :, :, 0:DL], c, AGC)
        for buf, kind in (
            (a_rel, A_REL), (a_dir, A_DIR), (a_sum, A_SUM), (a_z, A_Z),
            (b_z, B_Z), (b_rel, B_REL), (b_dir, B_DIR), (b_sum, B_SUM),
        ):
            sent(buf.at[c], c, kind)
        for rows, cols, kind in (
            (B, slice(0, WA), GA_Z), (4 * B, slice(0, WA), GA_1), (2 * B, slice(0, WA), GA_2),
            (2 * B, slice(WA, FH), GB_1), (B, slice(WA, FH), GB_2), (4 * B, slice(WA, FH), GB_Z),
        ):
            sent(hid.at[core, c, :, 0:rows, cols], c, kind)
        sent(hid.at[core, c, :, :, 0:WA], c, GC_A)
        sent(hid.at[core, c, :, :, WA:FH], c, GC_B)

    def s12(c):
        pl.when(c < NCH - 2)(lambda: settle(c))

    def s11(c):
        for k, chunks, first in ((4, (2, 3), 0), (5, (4,), HT)):

            @pl.when(c == k)
            def _(k=k, chunks=chunks, first=first):
                for chunk in chunks:
                    got(oc.at[chunk], chunk, RX)
                half = pl.ds(first, HT)
                total = oc[OTHER, :, half, :] + xr[1, 2, :, half, :]
                zs[:, half, :] = (total + xr[1, 0, :, half, :] + xr[1, 1, :, half, :]).astype(bf16)
                send(zs.at[:, half, :], zr.at[:, half, :], k, RZ, ZH)

        @pl.when(c == NCH - 1)
        def _():
            pl.loop(NCH - 2, NCH)(settle)
            for chunk in (0, 5):
                got(oc.at[chunk], chunk, RX)
            for k in (4, 5):
                got(zr.at[:, 0:HT, :], k, RZ)
            totals = [oc[NCH - 1, i] + xr[0, 2, i] + zr[i].astype(f32) for i in range(2)]
            for i, result in enumerate((mlp, ing)):
                result[0:HT, :] = (totals[i][0:HT] + xr[0, 0, i, 0:HT] + xr[0, 1, i, 0:HT]).astype(bf16)
            got(near6, 6, RX)
            for i, result in enumerate((mlp, ing)):
                both = xr6[0, i].astype(f32) + xr6[1, i].astype(f32)
                result[HT:TOK, :] = (totals[i][HT:TOK] + both).astype(bf16)

    for copy in takes:
        copy.wait()
    gather()
    for copy in swaps:
        copy.start()
    for copy in locals_:
        copy.start()

    order = (
        (9, s11), (7, s9a), (7, s9b), (6, s8a), (5, s7a), (6, s8b), (7, s10), (1, s3),
        (0, s2), (5, s7b), (4, s6a), (4, s6b), (2, s4b), (2, s4a), (3, s5a), (3, s5b),
        (10, s12),
    )

    @pl.loop(0, NCH + STAGES - 1)
    def _(t):
        @pl.when((t >= FIRST) & (t < LAST))
        def _():
            early(t)

        for stage, work in order:

            @pl.when((t >= stage) & (t < stage + NCH))
            def _(stage=stage, work=work):
                work(t - stage)

    for copy in swaps:
        copy.wait_send()


TILE = 512


def gradients(mlp0, ing0, xt, down, hidt, grads, p_in, p_out, mlp, ing, wig, wog, g_in, g_out, sem):
    copies = [
        pltpu.make_async_copy(mlp0, mlp, sem.at[0, 0]),
        pltpu.make_async_copy(ing0, ing, sem.at[1, 0]),
    ]
    for copy in copies:
        copy.start()
    for j in range(FL // TILE):
        units = pl.ds(j * TILE, TILE)
        g_out[units, :] = p_out[units, :] + jnp.dot(hidt[units, :], down[...], preferred_element_type=f32)
        g_in[:, units] = p_in[:, units] + jnp.dot(xt[...], grads[:, units], preferred_element_type=f32)
        for copy in (
            pltpu.make_async_copy(g_out.at[units, :], wog.at[units, :], sem.at[0, j + 1]),
            pltpu.make_async_copy(g_in.at[:, units], wig.at[:, units], sem.at[1, j + 1]),
        ):
            copy.start()
            copies.append(copy)
    for copy in copies:
        copy.wait()


def on_device(tokens, w_in, w_out, out_grad):
    vmem, anywhere = pl.BlockSpec(memory_space=pltpu.VMEM), pl.BlockSpec(memory_space=pl.ANY)
    scratch = [
        ((NCH, 2, C, DC), bf16),
        ((DC, FH), bf16),
        ((FH, DC), bf16),
        ((DL, FL), bf16),
        ((FL, DL), bf16),
        ((NCH, 2, C, FH), bf16),
        ((NCH, 2, 2 * B, WA), bf16),
        ((NCH, 2, 2 * B, WA), bf16),
        ((NCH, 2, 2 * B, WA), bf16),
        ((NCH, 2, B, WA), bf16),
        ((NCH, 2, B, WA), bf16),
        ((NCH, 2, 4 * B, WB), bf16),
        ((NCH, 2, B, WB), bf16),
        ((NCH, 2, B, WB), bf16),
        ((NCH, 2, B, WB), bf16),
        ((2, NCH, 2, C, FH), bf16),
        ((NCH, 2, C, DL), f32),
        ((2, 3, 2, TOK, DL), f32),
        ((2, C, DL), bf16),
        ((2, 2, HT, DL), bf16),
        ((2, TOK, DL), bf16),
        ((2, TOK, DL), bf16),
    ]
    handed = [
        ((TOK, DL), bf16),
        ((TOK, DL), bf16),
        ((DL, HALF), bf16),
        ((HALF, DL), bf16),
        ((FL, HALF), bf16),
        ((HALF, FL), bf16),
        ((DL, FL), f32),
        ((FL, DL), f32),
    ]
    between = pl.pallas_call(
        kernel,
        out_shape=tuple(pltpu.VMEM(shape, dtype) for shape, dtype in handed),
        in_specs=[anywhere] * 4,
        out_specs=(vmem,) * len(handed),
        scratch_shapes=[pltpu.VMEM(shape, dtype) for shape, dtype in scratch]
        + [
            pltpu.SemaphoreType.DMA((NCH, KINDS)),
            pltpu.SemaphoreType.DMA((NCH, KINDS)),
            pltpu.SemaphoreType.DMA((4,)),
            pltpu.SemaphoreType.DMA((6,)),
        ],
        compiler_params=pltpu.CompilerParams(
            collective_id=0, has_side_effects=True, vmem_limit_bytes=45 * 2**20
        ),
    )(tokens, out_grad, w_in, w_out)
    between = [pltpu.with_memory_space_constraint(v, pltpu.VMEM) for v in between]
    return pl.pallas_call(
        gradients,
        out_shape=(
            jax.ShapeDtypeStruct((TOK, DL), bf16),
            jax.ShapeDtypeStruct((TOK, DL), bf16),
            jax.ShapeDtypeStruct((DL, FL), f32),
            jax.ShapeDtypeStruct((FL, DL), f32),
        ),
        in_specs=[vmem] * len(handed),
        out_specs=(anywhere,) * 4,
        scratch_shapes=[
            pltpu.VMEM((DL, FL), f32),
            pltpu.VMEM((FL, DL), f32),
            pltpu.SemaphoreType.DMA((2, FL // TILE + 1)),
        ],
        compiler_params=pltpu.CompilerParams(vmem_limit_bytes=12 * 2**20),
    )(*between)


def solution(mesh):
    in_specs = (P("row", "col"), P("col", "row"), P("row", "col"), P("row", "col"))
    out_specs = (P("row", "col"), P("row", "col"), P("col", "row"), P("row", "col"))
    return jax.shard_map(
        on_device, mesh=mesh, in_specs=in_specs, out_specs=out_specs, check_vma=False
    )
```

```python
import jax
import jax.numpy as jnp
from jax import lax
from jax.experimental import pallas as pl
from jax.experimental.pallas import tpu as pltpu
from jax.sharding import PartitionSpec as P

MESH = pl.DeviceIdType.MESH
f32, bf16 = jnp.float32, jnp.bfloat16
sqrt_half = 0.7071067811865476
inv_root = 0.3989422804014327

ROWS = 8
TOK = 128
DL = 384
DC = 768
FL = 3072
FH = 1536
NCH = 8
B = TOK // NCH
C = B * ROWS
WA, WB = 1024, 512
HA, HB = -(-WA // 256) * 128, -(-WB // 256) * 128
HT = TOK // 2
NEAR = {0: 0, 2: 0, 4: HT, 6: HT}
FAR = (5, 3)
OTHER = 1
STAGES = 10
FIRST, LAST = 11, 15
HALF = NCH // 2 * C

(AGX, AGC, A_REL, A_DIR, A_SUM, A_Z, B_Z, B_REL, B_DIR, B_SUM, GA_Z, GA_1, GA_2, GB_1, GB_2, GB_Z, GC_A, GC_B, RX, RZ) = range(20)
KINDS = 20


def kernel(
    tok, dy, w_in, w_out,
    mlp, ing, xt, down, hidt, grads, p_in, p_out,
    xall, wih, woh, winv, woutv, part,
    a_rel, a_dir, a_sum, a_out, a_z, b_z, b_rel, b_dir, b_sum,
    hid, oc, xr, near6, xr6, zs, zr,
    ssem, rsem, wsem, lsem,
):
    row, col = lax.axis_index("row"), lax.axis_index("col")
    x, zh = row // 2, row % 2
    zl, y, core = col // 8, (col // 2) % 4, col % 2
    other = 1 - core

    def dev(dx=0, dzh=0, dzl=0, dyy=0, dc=0):
        return (
            ((x + dx) % 4) * 2 + (zh + dzh) % 2,
            (((zl + dzl) % 2) * 4 + (y + dyy) % 4) * 2 + (core + dc) % 2,
        )

    XP, XM, XO = dev(dx=1), dev(dx=3), dev(dx=2)
    ZH, ZL = dev(dzh=1), dev(dzl=1)
    YP, YM = dev(dyy=1), dev(dyy=3)
    CO = dev(dc=1)
    yr, yl, yo = (y + 1) % 4, (y + 3) % 4, (y + 2) % 4

    def send(src, dst, c, kind, to):
        pltpu.make_async_remote_copy(
            src_ref=src, dst_ref=dst, send_sem=ssem.at[c, kind], recv_sem=rsem.at[c, kind],
            device_id=to, device_id_type=MESH,
        ).start()

    def got(view, c, kind):
        pltpu.make_async_copy(view, view, rsem.at[c, kind]).wait()

    def sent(view, c, kind):
        pltpu.make_async_copy(view, view, ssem.at[c, kind]).wait()

    def ds(i, size):
        return pl.ds(pl.multiple_of(i * size, size), size)

    barrier = pltpu.get_barrier_semaphore()
    for d in (XP, XM, XO, ZH, ZL, YP, YM, CO):
        pl.semaphore_signal(barrier, 1, device_id=d, device_id_type=MESH)
    takes = [
        pltpu.make_async_copy(src, xall.at[NCH - 1, i, :, 0:DL], lsem.at[4 + i]) for i, src in enumerate((tok, dy))
    ]
    locals_ = [
        pltpu.make_async_copy(w_in.at[:, ds(core, FH)], wih.at[pl.ds(0, DL), :], lsem.at[0]),
        pltpu.make_async_copy(w_out.at[ds(core, FH), :], woh.at[:, pl.ds(0, DL)], lsem.at[1]),
        pltpu.make_async_copy(w_in, winv, lsem.at[2]),
        pltpu.make_async_copy(w_out, woutv, lsem.at[3]),
    ]
    for copy in takes + locals_:
        copy.start()
    pl.semaphore_wait(barrier, 8)

    swaps = [
        pltpu.make_async_remote_copy(
            src_ref=w_in.at[:, ds(other, FH)], dst_ref=wih.at[pl.ds(DL, DL), :],
            send_sem=wsem.at[0], recv_sem=wsem.at[1], device_id=CO, device_id_type=MESH,
        ),
        pltpu.make_async_remote_copy(
            src_ref=w_out.at[ds(other, FH), :], dst_ref=woh.at[:, pl.ds(DL, DL)],
            send_sem=wsem.at[2], recv_sem=wsem.at[3], device_id=CO, device_id_type=MESH,
        ),
    ]
    def near(c, src):
        half = pl.ds(NEAR[c], HT)
        send(xall.at[src, :, half, 0:DL], xall.at[c, :, pl.ds(0, HT), 0:DL], c, AGX, XM)
        send(xall.at[src, :, half, 0:DL], xall.at[c, :, pl.ds(HT, HT), 0:DL], c, AGX, XP)

    def whole(c, src, to):
        send(xall.at[src, :, :, 0:DL], xall.at[c, :, :, 0:DL], c, AGX, to)

    def gather():
        near(0, NCH - 1)
        whole(OTHER, NCH - 1, ZH)

    def forward():
        got(xall.at[OTHER, :, :, 0:DL], OTHER, AGX)
        near(2, OTHER)
        whole(FAR[1], OTHER, XO)
        near(4, OTHER)
        whole(FAR[0], NCH - 1, XO)
        near(6, NCH - 1)

    def s2(c):
        pl.when(c == OTHER)(forward)

        @pl.when((c != OTHER) & (c != NCH - 1))
        def _():
            got(xall.at[c, :, :, 0:DL], c, AGX)

        send(xall.at[c, :, :, 0:DL], xall.at[c, :, :, DL:DC], c, AGC, CO)

    def y_rows(d, rows, off):
        return pl.ds(pl.multiple_of(d * rows + off, B), rows)

    def y_send(c, rows, off, c0, cut, c1, rel, direct, krel, kdir):
        h = cut - c0
        for i, (half, place) in enumerate(((pl.ds(c0, h), pl.ds(0, h)), (pl.ds(cut, c1 - cut), pl.ds(h, c1 - cut)))):
            send(part.at[c, :, y_rows(yo, rows, off), half], rel.at[c, :, :, place], c, krel, (YP, YM)[i])
            d, to = ((yl, YM), (yr, YP))[i]
            send(part.at[c, :, y_rows(d, rows, off), half], direct.at[c, :, :, place], c, kdir, to)

    def y_relay(c, rows, off, c0, cut, c1, rel, total, krel, ksum):
        got(rel.at[c], c, krel)
        h = cut - c0
        for half, at, d, to in (
            (pl.ds(c0, h), pl.ds(0, h), yr, YP), (pl.ds(cut, c1 - cut), pl.ds(h, c1 - cut), yl, YM),
        ):
            place = (c, slice(None), y_rows(d, rows, off), half)
            part[place] = (part[place].astype(f32) + rel[c, :, :, at].astype(f32)).astype(bf16)
            send(part.at[place], total.at[c, :, :, at], c, ksum, to)

    def y_total(c, rows, off, sub, c0, c1, direct, total):
        own = part[c, :, pl.ds(pl.multiple_of(y * rows + off + sub, B), B), c0:c1]
        at = pl.ds(pl.multiple_of(sub, B), B)
        return own.astype(f32) + direct[c, :, at, :].astype(f32) + total[c, :, at, :].astype(f32)

    off_b = zl * (4 * B)
    route_a = (2 * B, 0, 0, HA, WA)
    route_b = (B, off_b, WA, WA + HB, FH)
    a_mine, b_mine = ds(y * 2 + zl, B), ds(zl * 4 + y, B)

    def s3(c):
        @pl.when(c == 0)
        def _():
            for copy in locals_[:2]:
                copy.wait()
            for copy in swaps:
                copy.wait_recv()

        got(xall.at[c, :, :, DL:DC], c, AGC)

        def products(first, end):
            @pl.loop(first, end)
            def _(j):
                cols = ds(j, 256)
                part[c, 0, :, cols] = jnp.dot(
                    xall[c, 0], wih[:, cols], preferred_element_type=f32
                ).astype(bf16)
                part[c, 1, :, cols] = lax.dot_general(
                    xall[c, 1], woh[cols, :], (((1,), (1,)), ((), ())), preferred_element_type=f32
                ).astype(bf16)

        products(0, -(-WA // 256))
        y_send(c, *route_a, a_rel, a_dir, A_REL, A_DIR)
        products(-(-WA // 256), FH // 256)
        send(part.at[c, :, ds(1 - zl, 4 * B), WA:FH], b_z.at[c], c, B_Z, ZL)

    def s4a(c):
        y_relay(c, *route_a, a_rel, a_sum, A_REL, A_SUM)

    def s4b(c):
        got(b_z.at[c], c, B_Z)
        place = (c, slice(None), ds(zl, 4 * B), slice(WA, FH))
        part[place] = (part[place].astype(f32) + b_z[c].astype(f32)).astype(bf16)
        y_send(c, *route_b, b_rel, b_dir, B_REL, B_DIR)

    def s5a(c):
        got(a_dir.at[c], c, A_DIR)
        got(a_sum.at[c], c, A_SUM)
        a_out[c] = y_total(c, 2 * B, 0, (1 - zl) * B, 0, WA, a_dir, a_sum).astype(bf16)
        send(a_out.at[c], a_z.at[c], c, A_Z, ZL)

    def s5b(c):
        y_relay(c, *route_b, b_rel, b_sum, B_REL, B_SUM)

    def unit(c, rows, c0, c1, both):
        pre, grad = both[0], both[1]
        half_erf = 0.5 * (1.0 + lax.erf(pre * sqrt_half))
        hid[core, c, 0, rows, c0:c1] = (pre * half_erf).astype(bf16)
        slope = half_erf + pre * jnp.exp(-0.5 * pre * pre) * inv_root
        hid[core, c, 1, rows, c0:c1] = (grad * slope).astype(bf16)

    def s6a(c):
        got(a_z.at[c], c, A_Z)
        unit(c, a_mine, 0, WA, y_total(c, 2 * B, 0, zl * B, 0, WA, a_dir, a_sum) + a_z[c].astype(f32))
        view = hid.at[core, c, :, a_mine, 0:WA]
        send(view, view, c, GA_Z, ZL)

    def s6b(c):
        got(b_dir.at[c], c, B_DIR)
        got(b_sum.at[c], c, B_SUM)
        unit(c, b_mine, WA, FH, y_total(c, B, off_b, 0, WA, FH, b_dir, b_sum))
        view = hid.at[core, c, :, b_mine, WA:FH]
        send(view, view, c, GB_1, YP)
        send(view, view, c, GB_1, YM)

    def y_forward(c, rows, off, c0, cut, c1, kind):
        for d, half, to in ((yl, pl.ds(c0, cut - c0), YP), (yr, pl.ds(cut, c1 - cut), YM)):
            view = hid.at[core, c, :, y_rows(d, rows, off), half]
            send(view, view, c, kind, to)

    def s7a(c):
        got(hid.at[core, c, :, ds(y * 2 + 1 - zl, B), 0:WA], c, GA_Z)
        view = hid.at[core, c, :, ds(y, 2 * B), 0:WA]
        send(view, view, c, GA_1, YP)
        send(view, view, c, GA_1, YM)

    def s7b(c):
        got(hid.at[core, c, :, 0 : 2 * B, WA:FH], c, GB_1)
        y_forward(c, *route_b, GB_2)

    def s8a(c):
        got(hid.at[core, c, :, 0 : 4 * B, 0:WA], c, GA_1)
        y_forward(c, *route_a, GA_2)

    def s8b(c):
        got(hid.at[core, c, :, 0:B, WA:FH], c, GB_2)
        view = hid.at[core, c, :, ds(zl, 4 * B), WA:FH]
        send(view, view, c, GB_Z, ZL)

    def s9a(c):
        got(hid.at[core, c, :, 0 : 2 * B, 0:WA], c, GA_2)
        send(hid.at[core, c, :, :, 0:WA], hid.at[core, c, :, :, 0:WA], c, GC_A, CO)

    def s9b(c):
        got(hid.at[core, c, :, 0 : 4 * B, WA:FH], c, GB_Z)
        send(hid.at[core, c, :, :, WA:FH], hid.at[core, c, :, :, WA:FH], c, GC_B, CO)

    def s10(c):
        @pl.when(c == 0)
        def _():
            for copy in locals_[2:]:
                copy.wait()

        def products(half):
            units = ds(half, FH)
            out = jnp.dot(hid[half, c, 0], woutv[units, :], preferred_element_type=f32)
            back = lax.dot_general(
                hid[half, c, 1], winv[:, units], (((1,), (1,)), ((), ())), preferred_element_type=f32
            )
            return out, back

        oc[c, 0], oc[c, 1] = products(core)
        got(hid.at[other, c, :, :, 0:WA], c, GC_A)
        got(hid.at[other, c, :, :, WA:FH], c, GC_B)
        out, back = products(other)
        oc[c, 0] += out
        oc[c, 1] += back
        for k, first in NEAR.items():
            if k == 6:
                continue

            @pl.when(c == k)
            def _(k=k, first=first):
                for i, to in enumerate((XP, XM)):
                    dst = xr.at[int(k in (2, 4)), i, :, pl.ds(first, HT), :]
                    send(oc.at[k, :, pl.ds(i * HT, HT), :], dst, k, RX, to)

        @pl.when(c == 6)
        def _():
            near6[...] = oc[6].astype(bf16)
            for i, to in enumerate((XP, XM)):
                send(near6.at[:, pl.ds(i * HT, HT), :], xr6.at[i], 6, RX, to)

        for k in FAR:

            @pl.when(c == k)
            def _(k=k):
                send(oc.at[k], xr.at[FAR.index(k), 2], k, RX, XO)

        @pl.when(c >= NCH // 2)
        def _():
            tokens = ds(c - NCH // 2, C)
            for k in range(2):
                hidt[k * FH : (k + 1) * FH, tokens] = hid[k, c, 0].T
                grads[tokens, k * FH : (k + 1) * FH] = hid[k, c, 1]
            xt[:, tokens] = xall[c, 0, :, 0:DL].T
            down[tokens, :] = xall[c, 1, :, 0:DL]

    def early(t):
        tiles = FL // 256 // (LAST - FIRST)
        first = pl.ds(0, NCH // 2)
        tn = (((0,), (0,)), ((), ()))
        up_t = xall[first, 0, :, 0:DL].reshape(HALF, DL).T

        @pl.loop(0, tiles)
        def _(i):
            j = (t - FIRST) * tiles + i
            units, k, place = ds(j, 256), j // 6, ds(j % 6, 256)
            p_out[units, :] = lax.dot_general(
                hid[k, first, 0, :, place].reshape(HALF, 256),
                xall[first, 1, :, 0:DL].reshape(HALF, DL),
                tn,
                preferred_element_type=f32,
            )
            p_in[:, units] = jnp.dot(
                up_t, hid[k, first, 1, :, place].reshape(HALF, 256), preferred_element_type=f32
            )

    def settle(c):
        @pl.when(c != NCH - 1)
        def _():
            sent(xall.at[c, :, :, 0:DL], c, AGX)

        @pl.when((c != NCH - 1) & (c != OTHER) & (c != 6))
        def _():
            sent(oc.at[c], c, RX)

        @pl.when(c == 6)
        def _():
            sent(near6, 6, RX)

        @pl.when((c == 5) | (c == 6))
        def _():
            sent(zr.at[:, 0:HT, :], c - 1, RZ)

        sent(xall.at[c, :, :, 0:DL], c, AGC)
        for buf, kind in (
            (a_rel, A_REL), (a_dir, A_DIR), (a_sum, A_SUM), (a_z, A_Z),
            (b_z, B_Z), (b_rel, B_REL), (b_dir, B_DIR), (b_sum, B_SUM),
        ):
            sent(buf.at[c], c, kind)
        for rows, cols, kind in (
            (B, slice(0, WA), GA_Z), (4 * B, slice(0, WA), GA_1), (2 * B, slice(0, WA), GA_2),
            (2 * B, slice(WA, FH), GB_1), (B, slice(WA, FH), GB_2), (4 * B, slice(WA, FH), GB_Z),
        ):
            sent(hid.at[core, c, :, 0:rows, cols], c, kind)
        sent(hid.at[core, c, :, :, 0:WA], c, GC_A)
        sent(hid.at[core, c, :, :, WA:FH], c, GC_B)

    def s12(c):
        pl.when(c < NCH - 2)(lambda: settle(c))

    def s11(c):
        for k, chunks, first in ((4, (2, 3), 0), (5, (4,), HT)):

            @pl.when(c == k)
            def _(k=k, chunks=chunks, first=first):
                for chunk in chunks:
                    got(oc.at[chunk], chunk, RX)
                half = pl.ds(first, HT)
                total = oc[OTHER, :, half, :] + xr[1, 2, :, half, :]
                zs[:, half, :] = (total + xr[1, 0, :, half, :] + xr[1, 1, :, half, :]).astype(bf16)
                send(zs.at[:, half, :], zr.at[:, half, :], k, RZ, ZH)

        @pl.when(c == NCH - 1)
        def _():
            pl.loop(NCH - 2, NCH)(settle)
            for chunk in (0, 5):
                got(oc.at[chunk], chunk, RX)
            for k in (4, 5):
                got(zr.at[:, 0:HT, :], k, RZ)
            totals = [oc[NCH - 1, i] + xr[0, 2, i] + zr[i].astype(f32) for i in range(2)]
            for i, result in enumerate((mlp, ing)):
                result[0:HT, :] = (totals[i][0:HT] + xr[0, 0, i, 0:HT] + xr[0, 1, i, 0:HT]).astype(bf16)
            got(near6, 6, RX)
            for i, result in enumerate((mlp, ing)):
                both = xr6[0, i].astype(f32) + xr6[1, i].astype(f32)
                result[HT:TOK, :] = (totals[i][HT:TOK] + both).astype(bf16)

    for copy in takes:
        copy.wait()
    gather()
    for copy in swaps:
        copy.start()

    order = (
        (9, s11), (7, s9a), (7, s9b), (6, s8a), (5, s7a), (6, s8b), (7, s10), (1, s3),
        (0, s2), (5, s7b), (4, s6a), (4, s6b), (2, s4b), (2, s4a), (3, s5a), (3, s5b),
        (10, s12),
    )

    @pl.loop(0, NCH + STAGES - 1)
    def _(t):
        @pl.when((t >= FIRST) & (t < LAST))
        def _():
            early(t)

        for stage, work in order:

            @pl.when((t >= stage) & (t < stage + NCH))
            def _(stage=stage, work=work):
                work(t - stage)

    for copy in swaps:
        copy.wait_send()


TILE = 512


def gradients(mlp0, ing0, xt, down, hidt, grads, p_in, p_out, mlp, ing, wig, wog, g_in, g_out, sem):
    copies = [
        pltpu.make_async_copy(mlp0, mlp, sem.at[0, 0]),
        pltpu.make_async_copy(ing0, ing, sem.at[1, 0]),
    ]
    for copy in copies:
        copy.start()
    for j in range(FL // TILE):
        units = pl.ds(j * TILE, TILE)
        g_out[units, :] = p_out[units, :] + jnp.dot(hidt[units, :], down[...], preferred_element_type=f32)
        g_in[:, units] = p_in[:, units] + jnp.dot(xt[...], grads[:, units], preferred_element_type=f32)
        for copy in (
            pltpu.make_async_copy(g_out.at[units, :], wog.at[units, :], sem.at[0, j + 1]),
            pltpu.make_async_copy(g_in.at[:, units], wig.at[:, units], sem.at[1, j + 1]),
        ):
            copy.start()
            copies.append(copy)
    for copy in copies:
        copy.wait()


def on_device(tokens, w_in, w_out, out_grad):
    vmem, anywhere = pl.BlockSpec(memory_space=pltpu.VMEM), pl.BlockSpec(memory_space=pl.ANY)
    scratch = [
        ((NCH, 2, C, DC), bf16),
        ((DC, FH), bf16),
        ((FH, DC), bf16),
        ((DL, FL), bf16),
        ((FL, DL), bf16),
        ((NCH, 2, C, FH), bf16),
        ((NCH, 2, 2 * B, WA), bf16),
        ((NCH, 2, 2 * B, WA), bf16),
        ((NCH, 2, 2 * B, WA), bf16),
        ((NCH, 2, B, WA), bf16),
        ((NCH, 2, B, WA), bf16),
        ((NCH, 2, 4 * B, WB), bf16),
        ((NCH, 2, B, WB), bf16),
        ((NCH, 2, B, WB), bf16),
        ((NCH, 2, B, WB), bf16),
        ((2, NCH, 2, C, FH), bf16),
        ((NCH, 2, C, DL), f32),
        ((2, 3, 2, TOK, DL), f32),
        ((2, C, DL), bf16),
        ((2, 2, HT, DL), bf16),
        ((2, TOK, DL), bf16),
        ((2, TOK, DL), bf16),
    ]
    handed = [
        ((TOK, DL), bf16),
        ((TOK, DL), bf16),
        ((DL, HALF), bf16),
        ((HALF, DL), bf16),
        ((FL, HALF), bf16),
        ((HALF, FL), bf16),
        ((DL, FL), f32),
        ((FL, DL), f32),
    ]
    between = pl.pallas_call(
        kernel,
        out_shape=tuple(pltpu.VMEM(shape, dtype) for shape, dtype in handed),
        in_specs=[anywhere] * 4,
        out_specs=(vmem,) * len(handed),
        scratch_shapes=[pltpu.VMEM(shape, dtype) for shape, dtype in scratch]
        + [
            pltpu.SemaphoreType.DMA((NCH, KINDS)),
            pltpu.SemaphoreType.DMA((NCH, KINDS)),
            pltpu.SemaphoreType.DMA((4,)),
            pltpu.SemaphoreType.DMA((6,)),
        ],
        compiler_params=pltpu.CompilerParams(
            collective_id=0, has_side_effects=True, vmem_limit_bytes=45 * 2**20
        ),
    )(tokens, out_grad, w_in, w_out)
    between = [pltpu.with_memory_space_constraint(v, pltpu.VMEM) for v in between]
    return pl.pallas_call(
        gradients,
        out_shape=(
            jax.ShapeDtypeStruct((TOK, DL), bf16),
            jax.ShapeDtypeStruct((TOK, DL), bf16),
            jax.ShapeDtypeStruct((DL, FL), f32),
            jax.ShapeDtypeStruct((FL, DL), f32),
        ),
        in_specs=[vmem] * len(handed),
        out_specs=(anywhere,) * 4,
        scratch_shapes=[
            pltpu.VMEM((DL, FL), f32),
            pltpu.VMEM((FL, DL), f32),
            pltpu.SemaphoreType.DMA((2, FL // TILE + 1)),
        ],
        compiler_params=pltpu.CompilerParams(vmem_limit_bytes=12 * 2**20),
    )(*between)


def solution(mesh):
    in_specs = (P("row", "col"), P("col", "row"), P("row", "col"), P("row", "col"))
    out_specs = (P("row", "col"), P("row", "col"), P("col", "row"), P("row", "col"))
    return jax.shard_map(
        on_device, mesh=mesh, in_specs=in_specs, out_specs=out_specs, check_vma=False
    )
```
